128 devices in a mesh: seq: 8 (over z, core), dp: 16 (over x, y).
Axes of the slice: x: 4, y: 4, z: 4, core: 2. Of those that a mesh axis runs over, the one named last changes fastest.
Arguments:
- hidden_rows: bfloat16 [16, 1024, 5120], P('dp', 'seq'), may hold values from -6 to 6
- segment_ids: int32 [16, 1024], P('dp'), may hold values from 0 to 7, never falling along the last dimension, each value on 1 to 512 neighbouring positions
- block_home: int32 [16, 64], P('dp'), may hold values from 0 to 63, as said below
- input_gain: float32 [5120], replicated, may hold values from 0.5 to 1.5
- w_query: bfloat16 [5120, 8192], P('dp', 'seq'), may hold values from -0.078125 to 0.078125
- key_weight: bfloat16 [5120, 1024], P('dp', 'seq'), may hold values from -0.078125 to 0.078125
- value_weight: bfloat16 [5120, 1024], P('dp', 'seq'), may hold values from -0.078125 to 0.078125
- q_gain: float32 [128], replicated, may hold values from 0.5 to 1.5
- k_gain: float32 [128], replicated, may hold values from 0.5 to 1.5
Outputs:
- moved_context: bfloat16 [16, 1024, 8192], P('dp', 'seq')
The draws below stay inside these ranges and needn't reach their ends.
Inputs may be any that keep to these rules, and one draw needn't show every extreme that they name: `block_home`: for each pack the entries are a permutation of the pack's block numbers; block b of the pack, as it lies in hidden_rows, is on device b // 8 of seq, and block position n lands on device n // 8; every device of seq receives exactly one block from each device of seq. `segment_ids`: never falling along a pack; each of the 8 documents has 1 to 512 positions.
All inputs are finite; a program needn't handle non-finite values.
Results may differ from the reference program's by a relative error of at most 0.0078.
Values may be sent and summed in bfloat16 or wider, within the bound.
A program may use at most 128 MiB of HBM per device.

```python
import math
import jax
import jax.numpy as jnp
import numpy as np
from jax import lax

MODEL_WIDTH = 5120
QUERY_HEADS = 64
KEY_VALUE_HEADS = 8
HEAD_SIZE = 128
NDOC = 8
PACK_LENGTH = 1024
PACKS = 16
BLK = 16
N_SEQ = 8


def latin_order(key):
    several = jax.random.split(key, 4)
    row_shift = jax.random.permutation(several[0], N_SEQ)
    col_shift = jax.random.permutation(several[1], N_SEQ)
    slot_shift = jax.random.randint(several[2], (N_SEQ,), 0, N_SEQ)
    slot_order = jax.random.permutation(several[3], N_SEQ)
    target = jnp.arange(N_SEQ, dtype=jnp.int32)[:, None]
    position = jnp.arange(N_SEQ, dtype=jnp.int32)[None, :]
    source = (row_shift[target] + col_shift[position]) % N_SEQ
    source_slot = slot_order[(target + slot_shift[source]) % N_SEQ]
    return (source * N_SEQ + source_slot).reshape(-1).astype(jnp.int32)


def draw_block_home(key, part):
    key = jax.random.fold_in(key, 11)
    pack_keys = jax.random.split(key, PACKS)
    return jax.vmap(latin_order)(pack_keys).astype(jnp.int32)


def block_levels(key, dims, cuts, least, top_value):
    def one(axis_at, blocks):
        heights = jax.random.uniform(jax.random.fold_in(jax.random.fold_in(key, 6), axis_at), (blocks,), jnp.float32, least / len(cuts), top_value / len(cuts))
        return jnp.repeat(jnp.exp(heights), dims[axis_at] // blocks).reshape((-1,) + (1,) * (len(dims) - axis_at - 1))

    factor_of = one(*cuts[0])
    for cut in cuts[1:]:
        factor_of = factor_of * one(*cut)
    return factor_of


def length_profile(amount, total, most, skew):
    weights = [(1 << 20) // math.isqrt(rank ** skew) + 1 for rank in range(2, amount + 1)]
    surplus, holding = total - most - (amount - 1), [1] * (amount - 1)
    while surplus > 0:
        movable = [i for i in range(amount - 1) if holding[i] < most]
        whole, budget = sum([weights[i] for i in movable]), surplus
        for i in movable:
            extra = min(most - holding[i], max(1, budget * weights[i] // whole), surplus)
            holding[i] = holding[i] + extra
            surplus = surplus - extra
    return np.array([most] + holding)


def uneven_parts(rng, count, total, reach, skew):
    if count == 2:
        one = jax.random.randint(rng, (), max(1, total - reach), min(reach, total - 1) + 1)
        return jnp.stack([one, total - one])
    sizes = jnp.asarray(length_profile(count, total, reach, skew), jnp.int32)
    pairs = (count - 1) // 2
    source_of, receiver = sizes[1:1 + 2 * pairs:2], sizes[2:2 + 2 * pairs:2]
    room = jnp.minimum(source_of - 1, reach - receiver)
    passed = jax.random.randint(jax.random.fold_in(rng, 1), (pairs,), 0, 1 << 20) % (room + 1)
    sizes = sizes.at[1:1 + 2 * pairs:2].set(source_of - passed).at[2:2 + 2 * pairs:2].set(receiver + passed)
    return sizes[jax.random.permutation(jax.random.fold_in(rng, 2), count)]


def normal_values(key, extent, spread, limit, pieces=(), kind=jnp.bfloat16):
    array = jax.random.normal(key, extent, jnp.float32) * spread
    if len(pieces) > 0:
        array = block_levels(key, extent, pieces, -0.22, 0.18) * array
    return jnp.clip(array, min=-limit, max=limit).astype(kind)


def setup_inputs(seed: int = 0) -> dict:
    key_of = jax.random.split(jax.random.key(seed), 10)
    return {
        "hidden_rows": normal_values(key_of[0], (PACKS, PACK_LENGTH, MODEL_WIDTH), 1.0, 6.0, ((0, 16), (1, 8))),
        "segment_ids": jax.vmap(lambda own: jnp.searchsorted(jnp.cumsum(uneven_parts(own, NDOC, PACK_LENGTH, PACK_LENGTH // 2, 2)), jnp.arange(PACK_LENGTH), side="right"))(jax.random.split(key_of[1], PACKS)).reshape((PACKS, PACK_LENGTH)).astype(jnp.int32),
        "block_home": draw_block_home(jax.random.fold_in(key_of[9], 71), 0),
        "input_gain": jnp.clip(jax.random.uniform(key_of[3], (MODEL_WIDTH,), jnp.float32, 0.5, 1.5), 0.5, 1.5),
        "w_query": normal_values(key_of[4], (MODEL_WIDTH, QUERY_HEADS * HEAD_SIZE), MODEL_WIDTH ** -0.5, 0.078125, ((0, 16), (1, 8))),
        "key_weight": normal_values(key_of[5], (MODEL_WIDTH, KEY_VALUE_HEADS * HEAD_SIZE), MODEL_WIDTH ** -0.5, 0.078125, ((0, 16), (1, 8))),
        "value_weight": normal_values(key_of[6], (MODEL_WIDTH, KEY_VALUE_HEADS * HEAD_SIZE), MODEL_WIDTH ** -0.5, 0.078125, ((0, 16), (1, 8))),
        "q_gain": jnp.clip(jax.random.uniform(key_of[7], (HEAD_SIZE,), jnp.float32, 0.5, 1.5), 0.5, 1.5),
        "k_gain": jnp.clip(jax.random.uniform(key_of[8], (HEAD_SIZE,), jnp.float32, 0.5, 1.5), 0.5, 1.5),
    }


EPS = 1e-06
ROPE_BASE = 1000000.0

def doc_positions(segments):
    row_index = jnp.arange(segments.shape[0], dtype=jnp.int32)
    previous = jnp.concatenate([segments[:1] - 1, segments[:-1]])
    starts = jnp.where(segments != previous, row_index, 0)
    return (row_index - lax.cummax(starts, axis=0)).astype(jnp.float32)

def rotary(value_rows, positions):
    half_dim = value_rows.shape[-1] // 2
    exponent = jnp.arange(half_dim, dtype=jnp.float32) * (2.0 / value_rows.shape[-1])
    frequency = jnp.exp(-math.log(ROPE_BASE) * exponent)
    angles = positions[:, None] * frequency[None, :]
    cosine = jnp.cos(angles)[:, None, :]
    sine_table = jnp.sin(angles)[:, None, :]
    first_half = value_rows[..., :half_dim]
    second = value_rows[..., half_dim:]
    return jnp.concatenate([first_half * cosine - second * sine_table, second * cosine + first_half * sine_table], axis=-1)

def head_norm(value_rows, head_gain):
    mean_square = lax.optimization_barrier(jnp.mean(value_rows * value_rows, axis=-1, keepdims=True))
    return value_rows * lax.rsqrt(mean_square + EPS) * head_gain

def reference(hidden_rows, segment_ids, block_home, input_gain, w_query, key_weight, value_weight, q_gain, k_gain):
    score_scale = 1.0 / math.sqrt(HEAD_SIZE)
    key_value_for_head = jnp.arange(QUERY_HEADS, dtype=jnp.int32) // (QUERY_HEADS // KEY_VALUE_HEADS)

    def one_pack(inputs):
        pack_rows, segments, new_order = inputs
        rows_wide = pack_rows.astype(jnp.float32)
        scale_rows = lax.rsqrt(lax.optimization_barrier(jnp.mean(rows_wide * rows_wide, axis=-1, keepdims=True)) + EPS)
        normalized_input = (rows_wide * scale_rows * input_gain).astype(jnp.bfloat16)
        query_raw = jnp.dot(normalized_input, w_query, preferred_element_type=jnp.float32).reshape(PACK_LENGTH, QUERY_HEADS, HEAD_SIZE)
        unnormed_key = jnp.dot(normalized_input, key_weight, preferred_element_type=jnp.float32).reshape(PACK_LENGTH, KEY_VALUE_HEADS, HEAD_SIZE)
        value_rows = jnp.dot(normalized_input, value_weight, preferred_element_type=jnp.float32).astype(jnp.bfloat16).reshape(PACK_LENGTH, KEY_VALUE_HEADS, HEAD_SIZE)
        positions = doc_positions(segments)
        queries = rotary(head_norm(query_raw, q_gain), positions).astype(jnp.bfloat16)
        keys_all = rotary(head_norm(unnormed_key, k_gain), positions).astype(jnp.bfloat16)
        row_index = jnp.arange(PACK_LENGTH, dtype=jnp.int32)
        allowed = (segments[:, None] == segments[None, :]) & (row_index[None, :] <= row_index[:, None])

        def one_head(head_inputs):
            head_query, kv_pick = head_inputs
            head_key = jnp.take(keys_all, kv_pick, axis=1)
            head_value = jnp.take(value_rows, kv_pick, axis=1)
            scores = jnp.dot(head_query, head_key.T, preferred_element_type=jnp.float32) * score_scale
            weights = jnp.where(allowed, jnp.exp(scores), 0.0)
            totals = lax.optimization_barrier(jnp.sum(weights, axis=-1, keepdims=True))
            mixed = jnp.dot(weights.astype(jnp.bfloat16), head_value, preferred_element_type=jnp.float32) / totals
            return mixed.astype(jnp.bfloat16)
        per_head = lax.map(one_head, (jnp.transpose(queries, (1, 0, 2)), key_value_for_head))
        context = jnp.transpose(per_head, (1, 0, 2)).reshape(PACK_LENGTH // BLK, BLK, QUERY_HEADS * HEAD_SIZE)
        return jnp.take(context, new_order, axis=0).reshape(PACK_LENGTH, QUERY_HEADS * HEAD_SIZE)
    return lax.map(one_pack, (hidden_rows, segment_ids, block_home))
```

```python
import math

import jax
import jax.numpy as jnp
from jax import lax
from jax.experimental import pallas as pl
from jax.experimental.pallas import tpu as pltpu
from jax.sharding import PartitionSpec as P

EPS = 1e-06
ROPE_BASE = 1000000.0
MESH = pl.DeviceIdType.MESH

SIDE = 4
SEQ = 8
ROWS = 1024
OWN = ROWS // SEQ
PIECE = OWN // 2
WIDTH = 5120
SHARD = WIDTH // (SIDE * SIDE)
HALF = SHARD // 2
HEAD = 128
WIDE = 2 * HEAD
CHUNKS = 5
HEADS_OUT = 1024
BLK = 16
BLOCKS = ROWS // BLK
QROWS = 256
BAND = 768
MASKED = -1e30
SCALE = math.log2(math.e) / math.sqrt(HEAD)


def place():
    s, d = lax.axis_index("seq"), lax.axis_index("dp")
    return s, d, d // SIDE, d % SIDE


def remote(src, dst, send, recv, seq, dp):
    return pltpu.make_async_remote_copy(
        src_ref=src,
        dst_ref=dst,
        send_sem=send,
        recv_sem=recv,
        device_id={"seq": seq, "dp": dp},
        device_id_type=MESH,
    )


def along(ring, step):
    _, _, x, y = place()
    if ring == 0:
        pos = (x + step + SIDE) % SIDE
        return pos * SIDE + y, pos
    pos = (y + step + SIDE) % SIDE
    return x * SIDE + pos, pos


FIRST = ((0, None, 1), (0, None, -1), (-1, 0, 1), (1, 1, -1))
SECOND = ((0, 0, 1), (0, 1, 1), (-1, 0, 1), (0, 1, -1), (0, 0, -1), (1, 1, -1))


def first_copy(b, j, half, kind, receiving=False):
    s, _, x, y = place()
    whose, part, way = FIRST[kind]
    target, _ = along(half, way)
    _, pos = along(half, whose - way if receiving else whose)
    rows = pl.ds(0, HALF) if part is None else pl.ds(part * (HALF // 2), HALF // 2)
    view = b.weights.at[j, pos, y, 0, rows] if half == 0 else b.weights.at[j, x, pos, 1, rows]
    return remote(view, view, b.first_send.at[j, half, kind], b.first_recv.at[j, half, kind], s, target)


def second_copy(b, j, half, kind, receiving=False):
    s, _, _, _ = place()
    whose, part, way = SECOND[kind]
    ring = 1 - half
    target, _ = along(ring, way)
    _, pos = along(ring, whose - way if receiving else whose)
    line = pl.ds(2 * part, 2)
    view = b.weights.at[j, line, pos, 0] if half == 0 else b.weights.at[j, pos, line, 1]
    return remote(view, view, b.second_send.at[j, half, kind], b.second_recv.at[j, half, kind], s, target)


def shard_rows(b, owner, part):
    if part is None:
        return b.rows.at[pl.ds(pl.multiple_of(owner * OWN, OWN), OWN)]
    return b.rows.at[pl.ds(pl.multiple_of(owner * OWN + part * PIECE, PIECE), PIECE)]


def row_copy(b, kind, receiving=False):
    s, d, _, _ = place()
    whose, part, way = SECOND[kind]
    target = (s + 2 * way + SEQ) % SEQ
    owner = (s + 2 * (whose - way if receiving else whose) + 2 * SEQ) % SEQ
    view = shard_rows(b, owner, part)
    return remote(view, view, b.row_send.at[kind], b.row_recv.at[kind], target, d)


def twin_copy(b, kind, receiving=False):
    s, d, _, _ = place()
    twin = s + 1 - 2 * (s % 2)
    base = twin if receiving else s
    if kind == 6:
        view = shard_rows(b, base, None)
    else:
        whose, part, way = SECOND[kind]
        view = shard_rows(b, (base + 2 * (whose - way) + 2 * SEQ) % SEQ, part)
    return remote(view, view, b.twin_send.at[kind], b.twin_recv.at[kind], twin, d)


def out_columns(b, owner, j):
    return b.out.at[0, :, pl.ds(pl.multiple_of(owner * HEADS_OUT + j * WIDE, WIDE), WIDE)]


def context_copy(b, j, step, receiving=False):
    s, d, _, _ = place()
    target = (s + step) % SEQ
    owner = (s - step + SEQ) % SEQ if receiving else s
    return remote(b.send.at[j, target], out_columns(b, owner, j), b.context_send.at[j, step - 1], b.context_recv.at[j, step - 1], target, d)


def own_context_copy(b, j):
    s, _, _, _ = place()
    return pltpu.make_async_copy(b.send.at[j, s], out_columns(b, s, j), b.local.at[j])


def own_weight_copies(b, j):
    _, _, x, y = place()
    mine = b.weights.at[j, x, y]
    if j == 0:
        return (
            pltpu.make_async_copy(b.key_weight, mine.at[:, :, pl.ds(0, HEAD)], b.own.at[0]),
            pltpu.make_async_copy(b.value_weight, mine.at[:, :, pl.ds(HEAD, HEAD)], b.own.at[1]),
        )
    return (pltpu.make_async_copy(b.w_query.at[:, :, pl.ds((j - 1) * WIDE, WIDE)], mine, b.own.at[j + 1]),)


def normalize(b):
    s, _, _, _ = place()

    @pl.loop(0, OWN // BLK)
    def _(i):
        at = pl.multiple_of(i * BLK, BLK)
        wide = b.hidden_here[pl.ds(at, BLK), :].astype(jnp.float32)
        scale = lax.rsqrt(jnp.mean(wide * wide, axis=-1, keepdims=True) + EPS)
        to = pl.multiple_of(s * OWN + at, BLK)
        b.rows[pl.ds(to, BLK), :] = (wide * scale * b.input_gain[...]).astype(jnp.bfloat16)


def tables(b):
    every = b.segments[...].astype(jnp.float32)
    counts = [jnp.sum(jnp.where(every == v, 1.0, 0.0), axis=1, keepdims=True) for v in range(SEQ - 1)]
    lane = lax.broadcasted_iota(jnp.int32, (1, HEAD), 1)
    exponent = (lane % (HEAD // 2)).astype(jnp.float32) * (2.0 / HEAD)
    frequency = jnp.exp(-math.log(ROPE_BASE) * exponent)
    sign = jnp.where(lane < HEAD // 2, -1.0, 1.0)
    down = lax.broadcasted_iota(jnp.int32, (HEAD, HEAD), 0)
    across = lax.broadcasted_iota(jnp.int32, (HEAD, HEAD), 1)
    step = lax.broadcasted_iota(jnp.int32, (HEAD, 1), 0)
    reach = lax.broadcasted_iota(jnp.int32, (HEAD, BAND), 1)

    @pl.loop(0, ROWS // HEAD)
    def _(i):
        at = pl.multiple_of(i * HEAD, HEAD)
        here = b.segments[:, pl.ds(at, HEAD)].astype(jnp.float32)
        column = jnp.sum(jnp.where(down == across, here, 0.0), axis=1, keepdims=True)
        start = jnp.zeros_like(column)
        for v, count in enumerate(counts):
            start = start + jnp.where(column > v, count, 0.0)
        place_of = (step + at).astype(jnp.float32)
        angle = (place_of - start) * frequency
        b.cosine[pl.ds(at, HEAD), :] = jnp.cos(angle)
        b.sine[pl.ds(at, HEAD), :] = jnp.sin(angle) * sign
        key = (reach + ((i // 2) * QROWS + QROWS - BAND)).astype(jnp.float32)
        allowed = (key >= start) & (key <= place_of)
        b.bias[pl.ds(at, HEAD), :] = jnp.where(allowed, 0.0, MASKED)


def turned(b, raw, gain, at):
    scale = lax.rsqrt(jnp.mean(raw * raw, axis=-1, keepdims=True) + EPS)
    normed = raw * scale * gain
    turn = normed * b.cosine[at, :] + pltpu.roll(normed, HEAD // 2, 1) * b.sine[at, :]
    return turn.astype(jnp.bfloat16)


def project(b, j, keys):
    piece = b.weights.at[j].reshape(WIDTH, WIDE)

    @pl.loop(0, ROWS // QROWS)
    def _(i):
        at = pl.ds(pl.multiple_of(i * QROWS, QROWS), QROWS)
        raw = jnp.dot(b.rows[at, :], piece[...], preferred_element_type=jnp.float32)
        if keys:
            b.keys[at, :] = turned(b, raw[:, :HEAD], b.k_gain[...], at)
            b.values[at, :] = raw[:, HEAD:].astype(jnp.bfloat16)
        else:
            for h in range(2):
                b.queries[h, at, :] = turned(b, raw[:, h * HEAD : (h + 1) * HEAD], b.q_gain[...], at)


def attend(b):
    @pl.loop(0, 2)
    def _(h):
        columns = pl.ds(pl.multiple_of(h * HEAD, HEAD), HEAD)
        for i in range(ROWS // QROWS):
            reach = min((i + 1) * QROWS, BAND)
            keys = pl.ds((i + 1) * QROWS - reach, reach)
            at = pl.ds(i * QROWS, QROWS)
            scores = lax.dot_general(
                b.queries[h, at, :], b.keys[keys, :], (((1,), (1,)), ((), ())), preferred_element_type=jnp.float32
            )
            weights = jnp.exp2(scores * SCALE + b.bias[at, BAND - reach :])
            total = jnp.sum(weights, axis=1, keepdims=True)
            mixed = jnp.dot(weights.astype(jnp.bfloat16), b.values[keys, :], preferred_element_type=jnp.float32)
            context = (mixed / total).astype(jnp.bfloat16)
            b.context[pl.ds(i * (QROWS // BLK), QROWS // BLK), :, columns] = context.reshape(QROWS // BLK, BLK, HEAD)


def reorder(b, j):
    per = BLOCKS // SEQ

    @pl.loop(0, SEQ)
    def _(t):
        for r in range(per):
            b.send[j, t, pl.ds(r * BLK, BLK), :] = b.context[b.home[0, t * per + r]]


def barrier():
    s, d, _, _ = place()
    ready = pltpu.get_barrier_semaphore()
    for ring in range(2):
        for step in (1, -1):
            target, _ = along(ring, step)
            pl.semaphore_signal(ready, inc=1, device_id={"seq": s, "dp": target}, device_id_type=MESH)
    for step in range(1, SEQ):
        pl.semaphore_signal(ready, inc=1, device_id={"seq": (s + step) % SEQ, "dp": d}, device_id_type=MESH)
    pl.semaphore_wait(ready, 4 + SEQ - 1)


def begin_second(b, j):
    for kind in (0, 3, 1, 4):
        for half in range(2):
            second_copy(b, j, half, kind).start()


def pass_second(b, j):
    for kind in (0, 3):
        for half in range(2):
            second_copy(b, j, half, kind, True).wait_recv()
            second_copy(b, j, half, kind + 2).start()


def finish_second(b, j):
    for kind in (1, 4, 2, 5):
        for half in range(2):
            second_copy(b, j, half, kind, True).wait_recv()


class Buffers:
    def __init__(self, names, refs):
        self.__dict__.update(zip(names, refs, strict=True))


SCRATCH = {
    "rows": pltpu.VMEM((ROWS, WIDTH), jnp.bfloat16),
    "weights": pltpu.VMEM((CHUNKS, SIDE, SIDE, 2, HALF, WIDE), jnp.bfloat16),
    "hidden_here": pltpu.VMEM((OWN, WIDTH), jnp.bfloat16),
    "cosine": pltpu.VMEM((ROWS, HEAD), jnp.float32),
    "sine": pltpu.VMEM((ROWS, HEAD), jnp.float32),
    "bias": pltpu.VMEM((ROWS, BAND), jnp.float32),
    "keys": pltpu.VMEM((ROWS, HEAD), jnp.bfloat16),
    "values": pltpu.VMEM((ROWS, HEAD), jnp.bfloat16),
    "queries": pltpu.VMEM((2, ROWS, HEAD), jnp.bfloat16),
    "context": pltpu.VMEM((BLOCKS, BLK, WIDE), jnp.bfloat16),
    "send": pltpu.VMEM((CHUNKS - 1, SEQ, OWN, WIDE), jnp.bfloat16),
    "own": pltpu.SemaphoreType.DMA((CHUNKS + 2,)),
    "local": pltpu.SemaphoreType.DMA((CHUNKS - 1,)),
    "first_send": pltpu.SemaphoreType.DMA((CHUNKS, 2, 4)),
    "first_recv": pltpu.SemaphoreType.DMA((CHUNKS, 2, 4)),
    "second_send": pltpu.SemaphoreType.DMA((CHUNKS, 2, 6)),
    "second_recv": pltpu.SemaphoreType.DMA((CHUNKS, 2, 6)),
    "row_send": pltpu.SemaphoreType.DMA((6,)),
    "row_recv": pltpu.SemaphoreType.DMA((6,)),
    "twin_send": pltpu.SemaphoreType.DMA((7,)),
    "twin_recv": pltpu.SemaphoreType.DMA((7,)),
    "context_send": pltpu.SemaphoreType.DMA((CHUNKS - 1, SEQ - 1)),
    "context_recv": pltpu.SemaphoreType.DMA((CHUNKS - 1, SEQ - 1)),
}
OPERANDS = ("hidden", "segments", "home", "input_gain", "q_gain", "k_gain", "w_query", "key_weight", "value_weight", "out")


def kernel(*refs):
    b = Buffers(OPERANDS + tuple(SCRATCH), refs)
    hidden_copy = pltpu.make_async_copy(b.hidden.at[0], b.hidden_here, b.own.at[CHUNKS + 1])
    hidden_copy.start()
    for j in range(CHUNKS):
        for copy in own_weight_copies(b, j):
            copy.start()
    barrier()

    for j in range(CHUNKS):
        for copy in own_weight_copies(b, j):
            copy.wait()
        for kind in (0, 1):
            for half in range(2):
                first_copy(b, j, half, kind).start()

    hidden_copy.wait()
    normalize(b)
    for kind in (0, 3, 1, 4):
        row_copy(b, kind).start()
    twin_copy(b, 6).start()

    @pl.loop(0, CHUNKS)
    def _(j):
        for kind in (0, 1):
            for half in range(2):
                first_copy(b, j, half, kind, True).wait_recv()
                first_copy(b, j, half, kind + 2).start()

    def finish_first(j):
        for kind in (2, 3):
            for half in range(2):
                first_copy(b, j, half, kind, True).wait_recv()

    finish_first(0)
    begin_second(b, 0)
    tables(b)
    for kind in (0, 3):
        row_copy(b, kind, True).wait_recv()
        row_copy(b, kind + 2).start()
        twin_copy(b, kind).start()
    for j in range(3):
        pass_second(b, j)
        finish_first(j + 1)
        begin_second(b, j + 1)
    for kind in (1, 4, 2, 5):
        row_copy(b, kind, True).wait_recv()
        twin_copy(b, kind).start()
    for kind in range(7):
        twin_copy(b, kind, True).wait_recv()

    finish_second(b, 0)
    project(b, 0, True)

    @pl.loop(1, CHUNKS)
    def _(j):
        finish_second(b, j)
        project(b, j, False)

        @pl.when(j == 1)
        def _():
            pass_second(b, 3)
            finish_first(4)
            begin_second(b, 4)

        @pl.when(j == 2)
        def _():
            pass_second(b, 4)

        attend(b)
        reorder(b, j - 1)
        for step in range(1, SEQ):
            context_copy(b, j - 1, step).start()
        own_context_copy(b, j - 1).start()

    @pl.loop(0, CHUNKS)
    def _(j):
        for half in range(2):
            for kind in range(4):
                first_copy(b, j, half, kind).wait_send()
            for kind in range(6):
                second_copy(b, j, half, kind).wait_send()

    for kind in range(6):
        row_copy(b, kind).wait_send()
    for kind in range(7):
        twin_copy(b, kind).wait_send()

    @pl.loop(0, CHUNKS - 1)
    def _(j):
        own_context_copy(b, j).wait()
        for step in range(1, SEQ):
            context_copy(b, j, step).wait_send()
            context_copy(b, j, step, True).wait_recv()


def body(hidden_rows, segment_ids, block_home, input_gain, w_query, key_weight, value_weight, q_gain, k_gain):
    anywhere = pl.BlockSpec(memory_space=pl.ANY)
    vector = pl.BlockSpec(memory_space=pltpu.VMEM)
    scalar = pl.BlockSpec(memory_space=pltpu.SMEM)
    return pl.pallas_call(
        kernel,
        out_shape=jax.ShapeDtypeStruct((1, OWN, SEQ * HEADS_OUT), jnp.bfloat16),
        in_specs=[anywhere, vector, scalar, vector, vector, vector, anywhere, anywhere, anywhere],
        out_specs=anywhere,
        scratch_shapes=list(SCRATCH.values()),
        compiler_params=pltpu.CompilerParams(
            collective_id=0, has_side_effects=True, vmem_limit_bytes=56 * 1024 * 1024
        ),
        name="packed_attention",
    )(
        hidden_rows,
        segment_ids,
        block_home,
        input_gain.reshape(1, WIDTH),
        q_gain.reshape(1, HEAD),
        k_gain.reshape(1, HEAD),
        w_query.reshape(2, HALF, HEADS_OUT),
        key_weight.reshape(2, HALF, HEAD),
        value_weight.reshape(2, HALF, HEAD),
    )


def solution(mesh):
    return jax.shard_map(
        body,
        mesh=mesh,
        in_specs=(
            P("dp", "seq", None),
            P("dp", None),
            P("dp", None),
            P(),
            P("dp", "seq"),
            P("dp", "seq"),
            P("dp", "seq"),
            P(),
            P(),
        ),
        out_specs=P("dp", "seq", None),
        check_vma=False,
    )
```

```python
import math

import jax
import jax.numpy as jnp
from jax import lax
from jax.experimental import pallas as pl
from jax.experimental.pallas import tpu as pltpu
from jax.sharding import PartitionSpec as P

EPS = 1e-06
ROPE_BASE = 1000000.0
MESH = pl.DeviceIdType.MESH

SIDE = 4
SEQ = 8
ROWS = 1024
OWN = ROWS // SEQ
PIECE = OWN // 2
WIDTH = 5120
SHARD = WIDTH // (SIDE * SIDE)
HALF = SHARD // 2
LINE = SIDE * HALF
LINES = 2 * SIDE
PIECES = LINES * SIDE
HEAD = 128
HEADS = 8
NDOC = 8
WIDE_CHUNKS = 4
NARROW_CHUNKS = 2
CHUNKS = WIDE_CHUNKS + NARROW_CHUNKS
BLK = 16
BLOCKS = ROWS // BLK
QROWS = 256
BAND = 768
MASKED = -1e30
SCALE = math.log2(math.e) / math.sqrt(HEAD)


def place():
    s, d = lax.axis_index("seq"), lax.axis_index("dp")
    return s, d, d // SIDE, d % SIDE


def remote(src, dst, send, recv, seq, dp):
    return pltpu.make_async_remote_copy(
        src_ref=src,
        dst_ref=dst,
        send_sem=send,
        recv_sem=recv,
        device_id={"seq": seq, "dp": dp},
        device_id_type=MESH,
    )


def along(ring, step):
    _, _, x, y = place()
    if ring == 0:
        pos = (x + step + SIDE) % SIDE
        return pos * SIDE + y, pos
    pos = (y + step + SIDE) % SIDE
    return x * SIDE + pos, pos


def chunk(b, j):
    return b.wide.at[j] if j < WIDE_CHUNKS else b.narrow.at[j - WIDE_CHUNKS]


def arrived(b, view, sem):
    s, d, _, _ = place()
    remote(view, view, b.context_send, sem, s, d).wait_recv()


def left(b, view, sem):
    s, d, _, _ = place()
    remote(view, view, sem, b.context_recv, s, d).wait_send()


FIRST = ((0, None, 1), (0, None, -1), (-1, 0, 1), (1, 1, -1))
SECOND = ((0, 0, 1), (0, 1, 1), (-1, 0, 1), (0, 1, -1), (0, 0, -1), (1, 1, -1))


def first_send(b, j, kind):
    s, _, x, y = place()
    whose, part, way = FIRST[kind]
    rows = pl.ds(0, HALF) if part is None else pl.ds(part * (HALF // 2), HALF // 2)
    for half in range(2):
        target, _ = along(half, way)
        _, pos = along(half, whose)
        line = half * SIDE + (y if half == 0 else x)
        view = chunk(b, j).at[line * SIDE + pos, rows]
        remote(view, view, b.weight_send.at[j], b.weight_recv.at[j, 0 if kind < 2 else 1], s, target).start()


def second_send(b, j, kind):
    s, _, _, _ = place()
    whose, part, way = SECOND[kind]
    for half in range(2):
        target, _ = along(1 - half, way)
        _, pos = along(1 - half, whose)
        view = chunk(b, j).at[pl.ds((half * SIDE + pos) * SIDE + 2 * part, 2)]
        sem = {0: 2, 3: 2, 1: 3, 4: 3, 2: 4, 5: 4}[kind]
        remote(view, view, b.weight_send.at[j], b.weight_recv.at[j, sem], s, target).start()


def begin_first(b, j):
    for kind in (0, 1):
        first_send(b, j, kind)


def pass_first(b, j):
    arrived(b, chunk(b, j).at[pl.ds(0, 4)], b.weight_recv.at[j, 0])
    for kind in (2, 3):
        first_send(b, j, kind)


def begin_second(b, j, part):
    if part == 0:
        arrived(b, chunk(b, j).at[pl.ds(0, 2)], b.weight_recv.at[j, 1])
    for kind in ((0, 3), (1, 4))[part]:
        second_send(b, j, kind)


def pass_second(b, j):
    arrived(b, chunk(b, j).at[pl.ds(0, 8)], b.weight_recv.at[j, 2])
    for kind in (2, 5):
        second_send(b, j, kind)
    if j + 1 < CHUNKS:
        begin_second(b, j + 1, 1)
    if j + 2 < CHUNKS:
        begin_second(b, j + 2, 0)


def rows_of(b, owner, part):
    if part is None:
        return b.rows.at[pl.ds(pl.multiple_of(owner * OWN, OWN), OWN)]
    return b.rows.at[pl.ds(pl.multiple_of(owner * OWN + part * PIECE, PIECE), PIECE)]


def row_send(b, kind):
    s, d, _, _ = place()
    whose, part, way = SECOND[kind]
    view = rows_of(b, (s + 2 * whose + SEQ) % SEQ, part)
    target = (s + 2 * way + SEQ) % SEQ
    remote(view, view, b.row_send, b.row_recv.at[{0: 0, 3: 0, 1: 1, 4: 1, 2: 2, 5: 2}[kind]], target, d).start()


def rows_arrived(b, group):
    s, d, _, _ = place()
    arrived(b, b.rows.at[pl.ds(0, OWN)], b.row_recv.at[group])
    if group == 0:
        for kind in (2, 5):
            row_send(b, kind)
    twin = s + 1 - 2 * (s % 2)
    for kind in ((0, 3), (1, 4), (2, 5))[group]:
        whose, part, way = SECOND[kind]
        view = rows_of(b, (s + 2 * (whose - way) + SEQ) % SEQ, part)
        remote(view, view, b.twin_send, b.twin_recv.at[group], twin, d).start()


def twin_arrived(b, group):
    arrived(b, b.rows.at[pl.ds(0, OWN)], b.twin_recv.at[group])


def begin_rows(b):
    s, d, _, _ = place()
    for kind in (0, 3, 1, 4):
        row_send(b, kind)
    twin = s + 1 - 2 * (s % 2)
    view = rows_of(b, s, None)
    remote(view, view, b.twin_send, b.twin_recv.at[3], twin, d).start()


def send_context(b, head):
    s, d, _, _ = place()
    columns = pl.ds(pl.multiple_of((s * HEADS + head) * HEAD, HEAD), HEAD)
    for step in range(1, SEQ):
        target = (s + step) % SEQ
        remote(b.send.at[head, target], b.out.at[0, :, columns], b.context_send, b.context_recv, target, d).start()
    pltpu.make_async_copy(b.send.at[head, s], b.out.at[0, :, columns], b.context_own).start()


def finish_context(b):
    arrived(b, b.send.at[:, pl.ds(0, SEQ - 1)], b.context_recv)
    left(b, b.send.at[:, pl.ds(0, SEQ - 1)], b.context_send)
    pltpu.make_async_copy(b.send.at[:, 0], b.send.at[:, 0], b.context_own).wait()


def begin_own(b, j):
    _, _, x, y = place()
    for half in range(2):
        mine = chunk(b, j).at[(half * SIDE + (y if half == 0 else x)) * SIDE + (x if half == 0 else y)]
        if j == 0:
            parts = ((b.key_weight.at[half], mine.at[:, pl.ds(0, HEAD)]), (b.value_weight.at[half], mine.at[:, pl.ds(HEAD, HEAD)]))
        else:
            size = 2 * HEAD if j < WIDE_CHUNKS else HEAD
            start = (j - 1) * 2 * HEAD if j < WIDE_CHUNKS else (WIDE_CHUNKS - 1) * 2 * HEAD + (j - WIDE_CHUNKS) * HEAD
            parts = ((b.w_query.at[half, :, pl.ds(start, size)], mine),)
        for src, dst in parts:
            pltpu.make_async_copy(src, dst, b.own.at[j]).start()


def finish_own(b, j):
    view = chunk(b, j).at[pl.ds(0, 2)]
    pltpu.make_async_copy(view, view, b.own.at[j]).wait()


def normalize(b):
    s, _, _, _ = place()

    @pl.loop(0, OWN // BLK)
    def _(i):
        at = pl.multiple_of(i * BLK, BLK)
        wide = b.hidden_here[pl.ds(at, BLK), :].astype(jnp.float32)
        scale = lax.rsqrt(jnp.mean(wide * wide, axis=-1, keepdims=True) + EPS)
        normed = wide * scale * b.input_gain[...]
        parts = [None] * PIECES
        for x in range(SIDE):
            for y in range(SIDE):
                start = (x * SIDE + y) * SHARD
                parts[y * SIDE + x] = normed[:, start : start + HALF]
                parts[(SIDE + x) * SIDE + y] = normed[:, start + HALF : start + SHARD]
        to = pl.multiple_of(s * OWN + at, BLK)
        b.rows[pl.ds(to, BLK), :] = jnp.concatenate(parts, axis=1).astype(jnp.bfloat16)


def tables(b):
    every = b.segments[...].astype(jnp.float32)
    counts = [jnp.sum(jnp.where(every == v, 1.0, 0.0), axis=1, keepdims=True) for v in range(NDOC - 1)]
    lane = lax.broadcasted_iota(jnp.int32, (1, HEAD), 1)
    exponent = (lane % (HEAD // 2)).astype(jnp.float32) * (2.0 / HEAD)
    frequency = jnp.exp(-math.log(ROPE_BASE) * exponent)
    sign = jnp.where(lane < HEAD // 2, -1.0, 1.0)
    down = lax.broadcasted_iota(jnp.int32, (HEAD, HEAD), 0)
    across = lax.broadcasted_iota(jnp.int32, (HEAD, HEAD), 1)
    step = lax.broadcasted_iota(jnp.int32, (HEAD, 1), 0)
    reach = lax.broadcasted_iota(jnp.int32, (HEAD, BAND), 1)

    @pl.loop(0, ROWS // HEAD)
    def _(i):
        at = pl.multiple_of(i * HEAD, HEAD)
        here = b.segments[:, pl.ds(at, HEAD)].astype(jnp.float32)
        column = jnp.sum(jnp.where(down == across, here, 0.0), axis=1, keepdims=True)
        start = jnp.zeros_like(column)
        for v, count in enumerate(counts):
            start = start + jnp.where(column > v, count, 0.0)
        place_of = (step + at).astype(jnp.float32)
        angle = (place_of - start) * frequency
        b.cosine[pl.ds(at, HEAD), :] = jnp.cos(angle)
        b.sine[pl.ds(at, HEAD), :] = jnp.sin(angle) * sign
        key = (reach + ((i // 2) * QROWS + QROWS - BAND)).astype(jnp.float32)
        allowed = (key >= start) & (key <= place_of)
        b.bias[pl.ds(at, HEAD), :] = jnp.where(allowed, 0.0, MASKED)


def turned(b, raw, gain, at):
    scale = lax.rsqrt(jnp.mean(raw * raw, axis=-1, keepdims=True) + EPS)
    normed = raw * scale * gain
    turn = normed * b.cosine[at, :] + pltpu.roll(normed, HEAD // 2, 1) * b.sine[at, :]
    return turn.astype(jnp.bfloat16)


def chip_rows(k):
    s, _, _, _ = place()
    return pl.ds(pl.multiple_of((s // 2 + k) % SIDE * QROWS, QROWS), QROWS)


def project_keys(b, at):
    raw = jnp.dot(b.rows[at, :], b.wide.at[0].reshape(WIDTH, 2 * HEAD)[...], preferred_element_type=jnp.float32)
    b.keys[at, :] = turned(b, raw[:, :HEAD], b.k_gain[...], at)
    b.values[at, :] = raw[:, HEAD:].astype(jnp.bfloat16)


def keep_queries(b, raw, at):
    for h in range(raw.shape[1] // HEAD):
        b.queries[h, at, :] = turned(b, raw[:, h * HEAD : (h + 1) * HEAD], b.q_gain[...], at)


def project_queries(b, at):
    raw = jnp.dot(b.rows[at, :], b.wide.at[1].reshape(WIDTH, 2 * HEAD)[...], preferred_element_type=jnp.float32)
    keep_queries(b, raw, at)


def lines_product(b, piece, at, late):
    _, _, x, y = place()
    left_sides, right_sides = [], []
    for half, mine in ((0, y), (1, x)):
        for step in (2,) if late else (0, 1, 3):
            line = half * SIDE + (mine + step) % SIDE
            left_sides.append(b.rows[at, pl.ds(pl.multiple_of(line * LINE, HEAD), LINE)])
            right_sides.append(piece[pl.ds(line * SIDE, SIDE)].reshape(LINE, piece.shape[-1]))
    return jnp.dot(
        jnp.concatenate(left_sides, axis=1), jnp.concatenate(right_sides, axis=0), preferred_element_type=jnp.float32
    )


def project_early(b, piece):
    columns = pl.ds(0, piece.shape[-1])
    for i in range(ROWS // QROWS):
        at = pl.ds(i * QROWS, QROWS)
        b.partial[at, columns] = lines_product(b, piece, at, False)


def project_late(b, piece):
    columns = pl.ds(0, piece.shape[-1])
    for i in range(ROWS // QROWS):
        at = pl.ds(i * QROWS, QROWS)
        keep_queries(b, b.partial[at, columns] + lines_product(b, piece, at, True), at)


def attend(b, slot, head):
    for i in range(ROWS // QROWS):
        reach = min((i + 1) * QROWS, BAND)
        keys = pl.ds((i + 1) * QROWS - reach, reach)
        at = pl.ds(i * QROWS, QROWS)
        scores = lax.dot_general(
            b.queries[slot, at, :], b.keys[keys, :], (((1,), (1,)), ((), ())), preferred_element_type=jnp.float32
        )
        weights = jnp.exp2(scores * SCALE + b.bias[at, BAND - reach :])
        total = jnp.sum(weights, axis=1, keepdims=True)
        mixed = jnp.dot(weights.astype(jnp.bfloat16), b.values[keys, :], preferred_element_type=jnp.float32)
        context = (mixed / total).astype(jnp.bfloat16)
        b.context[pl.ds(i * (QROWS // BLK), QROWS // BLK)] = context.reshape(QROWS // BLK, BLK, HEAD)
    per = BLOCKS // SEQ
    for t in range(SEQ):
        for r in range(per):
            b.send[head, t, pl.ds(r * BLK, BLK), :] = b.context[b.home[0, t * per + r]]
    send_context(b, head)


def barrier():
    s, d, _, _ = place()
    ready = pltpu.get_barrier_semaphore()
    for ring in range(2):
        for step in (1, -1):
            target, _ = along(ring, step)
            pl.semaphore_signal(ready, inc=1, device_id={"seq": s, "dp": target}, device_id_type=MESH)
    for step in range(1, SEQ):
        pl.semaphore_signal(ready, inc=1, device_id={"seq": (s + step) % SEQ, "dp": d}, device_id_type=MESH)
    pl.semaphore_wait(ready, 4 + SEQ - 1)


class Buffers:
    def __init__(self, names, refs):
        self.__dict__.update(zip(names, refs, strict=True))


SCRATCH = {
    "rows": pltpu.VMEM((ROWS, WIDTH), jnp.bfloat16),
    "wide": pltpu.VMEM((WIDE_CHUNKS, PIECES, HALF, 2 * HEAD), jnp.bfloat16),
    "narrow": pltpu.VMEM((NARROW_CHUNKS, PIECES, HALF, HEAD), jnp.bfloat16),
    "hidden_here": pltpu.VMEM((OWN, WIDTH), jnp.bfloat16),
    "segments": pltpu.VMEM((1, ROWS), jnp.int32),
    "home": pltpu.SMEM((1, BLOCKS), jnp.int32),
    "input_gain": pltpu.VMEM((1, WIDTH), jnp.float32),
    "q_gain": pltpu.VMEM((1, HEAD), jnp.float32),
    "k_gain": pltpu.VMEM((1, HEAD), jnp.float32),
    "cosine": pltpu.VMEM((ROWS, HEAD), jnp.float32),
    "sine": pltpu.VMEM((ROWS, HEAD), jnp.float32),
    "bias": pltpu.VMEM((ROWS, BAND), jnp.float32),
    "keys": pltpu.VMEM((ROWS, HEAD), jnp.bfloat16),
    "values": pltpu.VMEM((ROWS, HEAD), jnp.bfloat16),
    "queries": pltpu.VMEM((2, ROWS, HEAD), jnp.bfloat16),
    "partial": pltpu.VMEM((ROWS, 2 * HEAD), jnp.float32),
    "context": pltpu.VMEM((BLOCKS, BLK, HEAD), jnp.bfloat16),
    "send": pltpu.VMEM((HEADS, SEQ, OWN, HEAD), jnp.bfloat16),
    "small": pltpu.SemaphoreType.DMA((6,)),
    "own": pltpu.SemaphoreType.DMA((CHUNKS,)),
    "weight_send": pltpu.SemaphoreType.DMA((CHUNKS,)),
    "weight_recv": pltpu.SemaphoreType.DMA((CHUNKS, 5)),
    "row_send": pltpu.SemaphoreType.DMA,
    "row_recv": pltpu.SemaphoreType.DMA((3,)),
    "twin_send": pltpu.SemaphoreType.DMA,
    "twin_recv": pltpu.SemaphoreType.DMA((4,)),
    "context_send": pltpu.SemaphoreType.DMA,
    "context_recv": pltpu.SemaphoreType.DMA,
    "context_own": pltpu.SemaphoreType.DMA,
}
OPERANDS = (
    "hidden",
    "segments_in",
    "home_in",
    "input_gain_in",
    "q_gain_in",
    "k_gain_in",
    "w_query",
    "key_weight",
    "value_weight",
    "out",
)


def kernel(*refs):
    b = Buffers(OPERANDS + tuple(SCRATCH), refs)
    small = [
        pltpu.make_async_copy(src, dst, b.small.at[i])
        for i, (src, dst) in enumerate(
            (
                (b.hidden.at[0], b.hidden_here),
                (b.input_gain_in, b.input_gain),
                (b.segments_in, b.segments),
                (b.home_in, b.home),
                (b.q_gain_in, b.q_gain),
                (b.k_gain_in, b.k_gain),
            )
        )
    ]
    for j in range(CHUNKS):
        begin_own(b, j)
        if j == 0:
            for copy in small:
                copy.start()
    barrier()

    for j in range(CHUNKS):
        finish_own(b, j)
        begin_first(b, j)
    small[0].wait()
    small[1].wait()
    normalize(b)
    begin_rows(b)
    for copy in small[2:]:
        copy.wait()
    tables(b)
    for j in range(CHUNKS):
        pass_first(b, j)
    begin_second(b, 0, 0)
    begin_second(b, 0, 1)
    begin_second(b, 1, 0)
    rows_arrived(b, 0)
    pass_second(b, 0)
    pass_second(b, 1)
    rows_arrived(b, 1)

    for part in (3, 4):
        arrived(b, b.wide.at[0, pl.ds(0, 8)], b.weight_recv.at[0, part])
    for group in (3, 0, 1):
        twin_arrived(b, group)

    @pl.loop(0, SIDE - 1)
    def _(k):
        project_keys(b, chip_rows((k + 3) % SIDE))

    pass_second(b, 2)
    for part in (3, 4):
        arrived(b, b.wide.at[1, pl.ds(0, 8)], b.weight_recv.at[1, part])

    @pl.loop(0, SIDE - 1)
    def _(k):
        project_queries(b, chip_rows((k + 3) % SIDE))

    rows_arrived(b, 2)
    twin_arrived(b, 2)
    project_keys(b, chip_rows(2))
    project_queries(b, chip_rows(2))

    @pl.loop(0, 2)
    def _(h):
        attend(b, h, h)

    @pl.loop(2, WIDE_CHUNKS)
    def _(j):
        arrived(b, b.wide.at[j, pl.ds(0, 8)], b.weight_recv.at[j, 3])
        project_early(b, b.wide.at[j])

        @pl.when(j == 2)
        def _():
            pass_second(b, 3)

        @pl.when(j == 3)
        def _():
            pass_second(b, 4)

        arrived(b, b.wide.at[j, pl.ds(0, 8)], b.weight_recv.at[j, 4])
        project_late(b, b.wide.at[j])

        @pl.loop(0, 2)
        def _(h):
            attend(b, h, 2 * (j - 1) + h)

    @pl.loop(0, NARROW_CHUNKS)
    def _(n):
        arrived(b, b.narrow.at[n, pl.ds(0, 8)], b.weight_recv.at[WIDE_CHUNKS + n, 3])
        project_early(b, b.narrow.at[n])

        @pl.when(n == 0)
        def _():
            pass_second(b, 5)

        arrived(b, b.narrow.at[n, pl.ds(0, 8)], b.weight_recv.at[WIDE_CHUNKS + n, 4])
        project_late(b, b.narrow.at[n])
        attend(b, 0, 2 * (WIDE_CHUNKS - 1) + n)

    for j in range(CHUNKS):
        left(b, chunk(b, j).at[pl.ds(0, PIECES - 2)], b.weight_send.at[j])
    left(b, b.rows.at[pl.ds(0, 6 * PIECE)], b.row_send)
    left(b, b.rows.at[pl.ds(0, OWN + 6 * PIECE)], b.twin_send)
    finish_context(b)


def hand_over(src, dst, sems):
    part = OWN // 4
    copies = [
        pltpu.make_async_copy(src.at[:, pl.ds(i * part, part)], dst.at[:, pl.ds(i * part, part)], sems.at[i])
        for i in range(4)
    ]
    for copy in copies:
        copy.start()
    for copy in copies:
        copy.wait()


def body(hidden_rows, segment_ids, block_home, input_gain, w_query, key_weight, value_weight, q_gain, k_gain):
    anywhere = pl.BlockSpec(memory_space=pl.ANY)
    vector = pl.BlockSpec(memory_space=pltpu.VMEM)
    shape = (1, OWN, SEQ * HEADS * HEAD)
    moved = pl.pallas_call(
        kernel,
        out_shape=pltpu.VMEM(shape, jnp.bfloat16),
        in_specs=[anywhere] * 9,
        out_specs=vector,
        scratch_shapes=list(SCRATCH.values()),
        compiler_params=pltpu.CompilerParams(
            collective_id=0, has_side_effects=True, vmem_limit_bytes=52 * 1024 * 1024
        ),
        name="packed_attention",
    )(
        hidden_rows,
        segment_ids,
        block_home,
        input_gain.reshape(1, WIDTH),
        q_gain.reshape(1, HEAD),
        k_gain.reshape(1, HEAD),
        w_query.reshape(2, HALF, HEADS * HEAD),
        key_weight.reshape(2, HALF, HEAD),
        value_weight.reshape(2, HALF, HEAD),
    )
    return pl.pallas_call(
        hand_over,
        out_shape=jax.ShapeDtypeStruct(shape, jnp.bfloat16),
        in_specs=[vector],
        out_specs=anywhere,
        scratch_shapes=[pltpu.SemaphoreType.DMA((4,))],
        compiler_params=pltpu.CompilerParams(vmem_limit_bytes=4 * 1024 * 1024),
        name="hand_over",
    )(moved)


def solution(mesh):
    return jax.shard_map(
        body,
        mesh=mesh,
        in_specs=(
            P("dp", "seq", None),
            P("dp", None),
            P("dp", None),
            P(),
            P("dp", "seq"),
            P("dp", "seq"),
            P("dp", "seq"),
            P(),
            P(),
        ),
        out_specs=P("dp", "seq", None),
        check_vma=False,
    )
```

```python
import math

import jax
import jax.numpy as jnp
from jax import lax
from jax.experimental import pallas as pl
from jax.experimental.pallas import tpu as pltpu
from jax.sharding import PartitionSpec as P

EPS = 1e-06
ROPE_BASE = 1000000.0
MESH = pl.DeviceIdType.MESH

SIDE = 4
SEQ = 8
ROWS = 1024
OWN = ROWS // SEQ
PIECE = OWN // 2
WIDTH = 5120
SHARD = WIDTH // (SIDE * SIDE)
HALF = SHARD // 2
LINE = SIDE * HALF
LINES = 2 * SIDE
PIECES = LINES * SIDE
HEAD = 128
HEADS = 8
NDOC = 8
WIDE_CHUNKS = 4
NARROW_CHUNKS = 2
CHUNKS = WIDE_CHUNKS + NARROW_CHUNKS
BLK = 16
BLOCKS = ROWS // BLK
QROWS = 256
BAND = 768
MASKED = -1e30
SCALE = math.log2(math.e) / math.sqrt(HEAD)


def place():
    s, d = lax.axis_index("seq"), lax.axis_index("dp")
    return s, d, d // SIDE, d % SIDE


def remote(src, dst, send, recv, seq, dp):
    return pltpu.make_async_remote_copy(
        src_ref=src,
        dst_ref=dst,
        send_sem=send,
        recv_sem=recv,
        device_id={"seq": seq, "dp": dp},
        device_id_type=MESH,
    )


def along(ring, step):
    _, _, x, y = place()
    if ring == 0:
        pos = (x + step + SIDE) % SIDE
        return pos * SIDE + y, pos
    pos = (y + step + SIDE) % SIDE
    return x * SIDE + pos, pos


def chunk(b, j):
    if j < WIDE_CHUNKS:
        return b.wide.at[j]
    return b.wide.at[WIDE_CHUNKS, :, :, pl.ds((j - WIDE_CHUNKS) * HEAD, HEAD)]


def arrived(b, view, sem):
    s, d, _, _ = place()
    remote(view, view, b.context_send, sem, s, d).wait_recv()


def left(b, view, sem):
    s, d, _, _ = place()
    remote(view, view, sem, b.context_recv, s, d).wait_send()


FIRST = ((0, None, 1), (0, None, -1), (-1, 0, 1), (1, 1, -1))
SECOND = ((0, 0, 1), (0, 1, 1), (-1, 0, 1), (0, 1, -1), (0, 0, -1), (1, 1, -1))


def first_send(b, j, kind):
    s, _, x, y = place()
    whose, part, way = FIRST[kind]
    rows = pl.ds(0, HALF) if part is None else pl.ds(part * (HALF // 2), HALF // 2)
    for half in range(2):
        target, _ = along(half, way)
        _, pos = along(half, whose)
        line = half * SIDE + (y if half == 0 else x)
        view = chunk(b, j).at[line * SIDE + pos, rows]
        remote(view, view, b.weight_send.at[j], b.weight_recv.at[j, 0 if kind < 2 else 1], s, target).start()


def second_send(b, j, kind):
    s, _, _, _ = place()
    whose, part, way = SECOND[kind]
    for half in range(2):
        target, _ = along(1 - half, way)
        _, pos = along(1 - half, whose)
        view = chunk(b, j).at[pl.ds((half * SIDE + pos) * SIDE + 2 * part, 2)]
        sem = {0: 2, 3: 2, 1: 3, 4: 3, 2: 4, 5: 4}[kind]
        remote(view, view, b.weight_send.at[j], b.weight_recv.at[j, sem], s, target).start()


def begin_first(b, j):
    for kind in (0, 1):
        first_send(b, j, kind)


def pass_first(b, j):
    arrived(b, chunk(b, j).at[pl.ds(0, 4)], b.weight_recv.at[j, 0])
    for kind in (2, 3):
        first_send(b, j, kind)


def finish_first(b, j):
    arrived(b, chunk(b, j).at[pl.ds(0, 2)], b.weight_recv.at[j, 1])


def begin_second(b, j, part):
    for kind in ((0, 3), (1, 4))[part]:
        second_send(b, j, kind)


def pass_second(b, j):
    arrived(b, chunk(b, j).at[pl.ds(0, 8)], b.weight_recv.at[j, 2])
    for kind in (2, 5):
        second_send(b, j, kind)
    if j + 1 < CHUNKS:
        begin_second(b, j + 1, 1)
    if j + 2 < CHUNKS:
        begin_second(b, j + 2, 0)


def finish_second(b, j, part):
    arrived(b, chunk(b, j).at[pl.ds(0, 8)], b.weight_recv.at[j, 3 + part])


def rows_of(b, owner, part):
    if part is None:
        return b.rows.at[pl.ds(pl.multiple_of(owner * OWN, OWN), OWN)]
    return b.rows.at[pl.ds(pl.multiple_of(owner * OWN + part * PIECE, PIECE), PIECE)]


def row_send(b, kind):
    s, d, _, _ = place()
    whose, part, way = SECOND[kind]
    view = rows_of(b, (s + 2 * whose + SEQ) % SEQ, part)
    target = (s + 2 * way + SEQ) % SEQ
    remote(view, view, b.row_send, b.row_recv.at[{0: 0, 3: 0, 1: 1, 4: 1, 2: 2, 5: 2}[kind]], target, d).start()


def rows_arrived(b, group):
    s, d, _, _ = place()
    arrived(b, b.rows.at[pl.ds(0, OWN)], b.row_recv.at[group])
    if group == 0:
        for kind in (2, 5):
            row_send(b, kind)
    twin = s + 1 - 2 * (s % 2)
    for kind in ((0, 3), (1, 4), (2, 5))[group]:
        whose, part, way = SECOND[kind]
        view = rows_of(b, (s + 2 * (whose - way) + SEQ) % SEQ, part)
        remote(view, view, b.twin_send, b.twin_recv.at[group], twin, d).start()


def twin_arrived(b, group):
    arrived(b, b.rows.at[pl.ds(0, OWN)], b.twin_recv.at[group])


def begin_rows(b, part):
    s, d, _, _ = place()
    if part == 0:
        row_send(b, 0)
        return
    for kind in (3, 1, 4):
        row_send(b, kind)
    twin = s + 1 - 2 * (s % 2)
    view = rows_of(b, s, None)
    remote(view, view, b.twin_send, b.twin_recv.at[3], twin, d).start()


def send_context(b, head):
    s, d, _, _ = place()
    columns = pl.ds(pl.multiple_of((s * HEADS + head) * HEAD, HEAD), HEAD)
    for step in range(1, SEQ):
        target = (s + step) % SEQ
        remote(b.send.at[head, target], b.out.at[0, :, columns], b.context_send, b.context_recv, target, d).start()
    pltpu.make_async_copy(b.send.at[head, s], b.out.at[0, :, columns], b.context_own).start()


def finish_context(b):
    arrived(b, b.send.at[:, pl.ds(0, SEQ - 1)], b.context_recv)
    left(b, b.send.at[:, pl.ds(0, SEQ - 1)], b.context_send)
    pltpu.make_async_copy(b.send.at[:, 0], b.send.at[:, 0], b.context_own).wait()


def begin_own(b, j):
    _, _, x, y = place()
    for half in range(2):
        mine = chunk(b, j).at[(half * SIDE + (y if half == 0 else x)) * SIDE + (x if half == 0 else y)]
        if j == 0:
            parts = ((b.key_weight.at[half], mine.at[:, pl.ds(0, HEAD)]), (b.value_weight.at[half], mine.at[:, pl.ds(HEAD, HEAD)]))
        else:
            size = 2 * HEAD if j < WIDE_CHUNKS else HEAD
            start = (j - 1) * 2 * HEAD if j < WIDE_CHUNKS else (WIDE_CHUNKS - 1) * 2 * HEAD + (j - WIDE_CHUNKS) * HEAD
            parts = ((b.w_query.at[half, :, pl.ds(start, size)], mine),)
        for src, dst in parts:
            pltpu.make_async_copy(src, dst, b.own.at[j]).start()


def finish_own(b, j):
    view = chunk(b, j).at[pl.ds(0, 2)]
    pltpu.make_async_copy(view, view, b.own.at[j]).wait()


def normalize(b, part):
    s, _, _, _ = place()

    @pl.loop(part * PIECE // BLK, (part + 1) * PIECE // BLK)
    def _(i):
        at = pl.multiple_of(i * BLK, BLK)
        wide = b.hidden_here[pl.ds(at, BLK), :].astype(jnp.float32)
        scale = lax.rsqrt(jnp.mean(wide * wide, axis=-1, keepdims=True) + EPS)
        normed = wide * scale * b.input_gain[...]
        parts = [None] * PIECES
        for x in range(SIDE):
            for y in range(SIDE):
                start = (x * SIDE + y) * SHARD
                parts[y * SIDE + x] = normed[:, start : start + HALF]
                parts[(SIDE + x) * SIDE + y] = normed[:, start + HALF : start + SHARD]
        to = pl.multiple_of(s * OWN + at, BLK)
        b.rows[pl.ds(to, BLK), :] = jnp.concatenate(parts, axis=1).astype(jnp.bfloat16)


def tables(b):
    every = b.segments[...].astype(jnp.float32)
    counts = [jnp.sum(jnp.where(every == v, 1.0, 0.0), axis=1, keepdims=True) for v in range(NDOC - 1)]
    lane = lax.broadcasted_iota(jnp.int32, (1, HEAD), 1)
    exponent = (lane % (HEAD // 2)).astype(jnp.float32) * (2.0 / HEAD)
    frequency = jnp.exp(-math.log(ROPE_BASE) * exponent)
    sign = jnp.where(lane < HEAD // 2, -1.0, 1.0)
    down = lax.broadcasted_iota(jnp.int32, (HEAD, HEAD), 0)
    across = lax.broadcasted_iota(jnp.int32, (HEAD, HEAD), 1)
    step = lax.broadcasted_iota(jnp.int32, (HEAD, 1), 0)
    reach = lax.broadcasted_iota(jnp.int32, (HEAD, BAND), 1)

    @pl.loop(0, ROWS // HEAD)
    def _(i):
        at = pl.multiple_of(i * HEAD, HEAD)
        here = b.segments[:, pl.ds(at, HEAD)].astype(jnp.float32)
        column = jnp.sum(jnp.where(down == across, here, 0.0), axis=1, keepdims=True)
        start = jnp.zeros_like(column)
        for v, count in enumerate(counts):
            start = start + jnp.where(column > v, count, 0.0)
        place_of = (step + at).astype(jnp.float32)
        angle = (place_of - start) * frequency
        b.cosine[pl.ds(at, HEAD), :] = jnp.cos(angle)
        b.sine[pl.ds(at, HEAD), :] = jnp.sin(angle) * sign
        key = (reach + ((i // 2) * QROWS + QROWS - BAND)).astype(jnp.float32)
        allowed = (key >= start) & (key <= place_of)
        b.bias[pl.ds(at, HEAD), :] = jnp.where(allowed, 0.0, MASKED)


def turned(b, raw, gain, at):
    scale = lax.rsqrt(jnp.mean(raw * raw, axis=-1, keepdims=True) + EPS)
    normed = raw * scale * gain
    turn = normed * b.cosine[at, :] + pltpu.roll(normed, HEAD // 2, 1) * b.sine[at, :]
    return turn.astype(jnp.bfloat16)


def chip_rows(k):
    s, _, _, _ = place()
    return pl.ds(pl.multiple_of((s // 2 + k) % SIDE * QROWS, QROWS), QROWS)


def project_keys(b, at):
    raw = jnp.dot(b.rows[at, :], b.wide.at[0].reshape(WIDTH, 2 * HEAD)[...], preferred_element_type=jnp.float32)
    b.keys[at, :] = turned(b, raw[:, :HEAD], b.k_gain[...], at)
    b.values[at, :] = raw[:, HEAD:].astype(jnp.bfloat16)


def keep_queries(b, raw, at):
    for h in range(raw.shape[1] // HEAD):
        b.queries[h, at, :] = turned(b, raw[:, h * HEAD : (h + 1) * HEAD], b.q_gain[...], at)


def project_queries(b, j, at):
    raw = jnp.dot(b.rows[at, :], b.wide.at[j].reshape(WIDTH, 2 * HEAD)[...], preferred_element_type=jnp.float32)
    keep_queries(b, raw, at)


FIRST_LINES, NEXT_LINES, LAST_LINES = (0,), (1, 3), (2,)


def lines_product(b, piece, at, steps):
    _, _, x, y = place()
    left_sides, right_sides = [], []
    for half, mine in ((0, y), (1, x)):
        for step in steps:
            line = half * SIDE + (mine + step) % SIDE
            left_sides.append(b.rows[at, pl.ds(pl.multiple_of(line * LINE, HEAD), LINE)])
            right_sides.append(piece[pl.ds(line * SIDE, SIDE)].reshape(LINE, piece.shape[-1]))
    return jnp.dot(
        jnp.concatenate(left_sides, axis=1), jnp.concatenate(right_sides, axis=0), preferred_element_type=jnp.float32
    )


def project_early(b, piece, partial):
    for k in (3, 0, 1):
        at = chip_rows(k)
        partial[at, :] += lines_product(b, piece, at, NEXT_LINES)
    at = chip_rows(2)
    partial[at, :] = lines_product(b, piece, at, FIRST_LINES + NEXT_LINES)


def attend(b, heads, head, query):
    steps = ROWS // QROWS

    def reach_of(i):
        reach = min((i + 1) * QROWS, BAND)
        return reach, pl.ds((i + 1) * QROWS - reach, reach)

    def score(i):
        keys = b.keys[reach_of(i)[1], :]
        return lax.dot_general(query(i), keys, (((1,), (1,)), ((), ())), preferred_element_type=jnp.float32)

    def mix(i, scores):
        reach, keys = reach_of(i)
        bias = b.bias[pl.ds(i * QROWS, QROWS), BAND - reach :]
        weights = jnp.exp2(scores.reshape(heads, QROWS, reach) * SCALE + bias[None]).reshape(heads * QROWS, reach)
        total = jnp.sum(weights, axis=1, keepdims=True)
        mixed = jnp.dot(weights.astype(jnp.bfloat16), b.values[keys, :], preferred_element_type=jnp.float32)
        context = (mixed / total).astype(jnp.bfloat16).reshape(heads, QROWS // BLK, BLK, HEAD)
        for h in range(heads):
            b.context[h, pl.ds(i * (QROWS // BLK), QROWS // BLK)] = context[h]

    scores = score(0)
    for i in range(steps):
        later = score(i + 1) if i + 1 < steps else None
        mix(i, scores)
        scores = later

    per = BLOCKS // SEQ
    for h in range(heads):
        for t in range(SEQ):
            for r in range(per):
                b.send[head + h, t, pl.ds(r * BLK, BLK), :] = b.context[h, b.home[0, t * per + r]]
        send_context(b, head + h)


def attend_kept(b, heads, head):
    def query(i):
        at = pl.ds(i * QROWS, QROWS)
        if heads == 1:
            return b.queries[0, at, :]
        return jnp.concatenate([b.queries[h, at, :] for h in range(heads)], axis=0)

    attend(b, heads, head, query)


def project_late(b, piece, partial):
    for i in range(ROWS // QROWS):
        at = pl.ds(i * QROWS, QROWS)
        keep_queries(b, partial[at, :] + lines_product(b, piece, at, LAST_LINES), at)


def barrier():
    s, d, _, _ = place()
    ready = pltpu.get_barrier_semaphore()
    for ring in range(2):
        for step in (1, -1):
            target, _ = along(ring, step)
            pl.semaphore_signal(ready, inc=1, device_id={"seq": s, "dp": target}, device_id_type=MESH)
    for step in range(1, SEQ):
        pl.semaphore_signal(ready, inc=1, device_id={"seq": (s + step) % SEQ, "dp": d}, device_id_type=MESH)
    pl.semaphore_wait(ready, 4 + SEQ - 1)


class Buffers:
    def __init__(self, names, refs):
        self.__dict__.update(zip(names, refs, strict=True))


SCRATCH = {
    "rows": pltpu.VMEM((ROWS, WIDTH), jnp.bfloat16),
    "wide": pltpu.VMEM((WIDE_CHUNKS + 1, PIECES, HALF, 2 * HEAD), jnp.bfloat16),
    "hidden_here": pltpu.VMEM((OWN, WIDTH), jnp.bfloat16),
    "segments": pltpu.VMEM((1, ROWS), jnp.int32),
    "home": pltpu.SMEM((1, BLOCKS), jnp.int32),
    "input_gain": pltpu.VMEM((1, WIDTH), jnp.float32),
    "q_gain": pltpu.VMEM((1, HEAD), jnp.float32),
    "k_gain": pltpu.VMEM((1, HEAD), jnp.float32),
    "cosine": pltpu.VMEM((ROWS, HEAD), jnp.float32),
    "sine": pltpu.VMEM((ROWS, HEAD), jnp.float32),
    "bias": pltpu.VMEM((ROWS, BAND), jnp.float32),
    "keys": pltpu.VMEM((ROWS, HEAD), jnp.bfloat16),
    "values": pltpu.VMEM((ROWS, HEAD), jnp.bfloat16),
    "queries": pltpu.VMEM((2, ROWS, HEAD), jnp.bfloat16),
    "partial": pltpu.VMEM((WIDE_CHUNKS - 1, ROWS, 2 * HEAD), jnp.float32),
    "context": pltpu.VMEM((2, BLOCKS, BLK, HEAD), jnp.bfloat16),
    "send": pltpu.VMEM((HEADS, SEQ, OWN, HEAD), jnp.bfloat16),
    "small": pltpu.SemaphoreType.DMA((6,)),
    "own": pltpu.SemaphoreType.DMA((CHUNKS,)),
    "weight_send": pltpu.SemaphoreType.DMA((CHUNKS,)),
    "weight_recv": pltpu.SemaphoreType.DMA((CHUNKS, 5)),
    "row_send": pltpu.SemaphoreType.DMA,
    "row_recv": pltpu.SemaphoreType.DMA((3,)),
    "twin_send": pltpu.SemaphoreType.DMA,
    "twin_recv": pltpu.SemaphoreType.DMA((4,)),
    "context_send": pltpu.SemaphoreType.DMA,
    "context_recv": pltpu.SemaphoreType.DMA,
    "context_own": pltpu.SemaphoreType.DMA,
}
OPERANDS = (
    "hidden",
    "segments_in",
    "home_in",
    "input_gain_in",
    "q_gain_in",
    "k_gain_in",
    "w_query",
    "key_weight",
    "value_weight",
    "out",
)


def kernel(*refs):
    b = Buffers(OPERANDS + tuple(SCRATCH), refs)
    small = [
        pltpu.make_async_copy(src, dst, b.small.at[i])
        for i, (src, dst) in enumerate(
            (
                (b.hidden.at[0], b.hidden_here),
                (b.input_gain_in, b.input_gain),
                (b.segments_in, b.segments),
                (b.home_in, b.home),
                (b.q_gain_in, b.q_gain),
                (b.k_gain_in, b.k_gain),
            )
        )
    ]
    for j in range(CHUNKS):
        begin_own(b, j)
        if j == 0:
            for copy in small:
                copy.start()
    barrier()

    for j in range(CHUNKS):
        finish_own(b, j)
        begin_first(b, j)
    small[0].wait()
    small[1].wait()
    for part in range(2):
        normalize(b, part)
        begin_rows(b, part)
    for copy in small[2:]:
        copy.wait()
    tables(b)
    for j in range(CHUNKS):
        pass_first(b, j)
    finish_first(b, 0)
    begin_second(b, 0, 0)
    begin_second(b, 0, 1)
    finish_first(b, 1)
    begin_second(b, 1, 0)
    for j in range(2, CHUNKS):
        finish_first(b, j)
    rows_arrived(b, 0)
    pass_second(b, 0)
    pass_second(b, 1)
    rows_arrived(b, 1)

    for part in range(2):
        finish_second(b, 0, part)
    for group in (3, 0, 1):
        twin_arrived(b, group)

    @pl.loop(0, SIDE - 1)
    def _(k):
        at = chip_rows((k + 3) % SIDE)
        project_keys(b, at)
        for j in (3, 4):
            b.partial[j - 2, at, :] = lines_product(b, b.wide.at[j], at, FIRST_LINES)

    pass_second(b, 2)
    for part in range(2):
        finish_second(b, 1, part)

    @pl.loop(0, SIDE - 1)
    def _(k):
        project_queries(b, 1, chip_rows((k + 3) % SIDE))

    finish_second(b, 2, 0)

    @pl.loop(0, SIDE - 1)
    def _(k):
        at = chip_rows((k + 3) % SIDE)
        b.partial[0, at, :] = lines_product(b, b.wide.at[2], at, FIRST_LINES + NEXT_LINES)

    rows_arrived(b, 2)
    twin_arrived(b, 2)
    project_keys(b, chip_rows(2))
    project_queries(b, 1, chip_rows(2))
    attend_kept(b, 2, 0)

    pass_second(b, 3)
    finish_second(b, 2, 1)
    for k in (3, 0, 1):
        at = chip_rows(k)
        keep_queries(b, b.partial[0, at, :] + lines_product(b, b.wide.at[2], at, LAST_LINES), at)
    project_queries(b, 2, chip_rows(2))
    attend_kept(b, 2, 2)

    finish_second(b, 3, 0)
    project_early(b, b.wide.at[3], b.partial.at[1])
    pass_second(b, 4)
    finish_second(b, 3, 1)
    project_late(b, b.wide.at[3], b.partial.at[1])
    attend_kept(b, 2, 4)

    for j in range(WIDE_CHUNKS, CHUNKS):
        finish_second(b, j, 0)
        partial = b.partial.at[2, :, pl.ds((j - WIDE_CHUNKS) * HEAD, HEAD)]
        project_early(b, chunk(b, j), partial)
        if j + 1 < CHUNKS:
            pass_second(b, j + 1)
        finish_second(b, j, 1)
        project_late(b, chunk(b, j), partial)
        attend_kept(b, 1, j + 2)

    for j in range(CHUNKS):
        left(b, chunk(b, j).at[pl.ds(0, PIECES - 2)], b.weight_send.at[j])
    left(b, b.rows.at[pl.ds(0, 6 * PIECE)], b.row_send)
    left(b, b.rows.at[pl.ds(0, OWN + 6 * PIECE)], b.twin_send)
    finish_context(b)


def hand_over(src, dst, sems):
    part = OWN // 4
    copies = [
        pltpu.make_async_copy(src.at[:, pl.ds(i * part, part)], dst.at[:, pl.ds(i * part, part)], sems.at[i])
        for i in range(4)
    ]
    for copy in copies:
        copy.start()
    for copy in copies:
        copy.wait()


def body(hidden_rows, segment_ids, block_home, input_gain, w_query, key_weight, value_weight, q_gain, k_gain):
    anywhere = pl.BlockSpec(memory_space=pl.ANY)
    vector = pl.BlockSpec(memory_space=pltpu.VMEM)
    shape = (1, OWN, SEQ * HEADS * HEAD)
    moved = pl.pallas_call(
        kernel,
        out_shape=pltpu.VMEM(shape, jnp.bfloat16),
        in_specs=[anywhere] * 9,
        out_specs=vector,
        scratch_shapes=list(SCRATCH.values()),
        compiler_params=pltpu.CompilerParams(
            collective_id=0, has_side_effects=True, vmem_limit_bytes=52 * 1024 * 1024
        ),
        name="packed_attention",
    )(
        hidden_rows,
        segment_ids,
        block_home,
        input_gain.reshape(1, WIDTH),
        q_gain.reshape(1, HEAD),
        k_gain.reshape(1, HEAD),
        w_query.reshape(2, HALF, HEADS * HEAD),
        key_weight.reshape(2, HALF, HEAD),
        value_weight.reshape(2, HALF, HEAD),
    )
    return pl.pallas_call(
        hand_over,
        out_shape=jax.ShapeDtypeStruct(shape, jnp.bfloat16),
        in_specs=[vector],
        out_specs=anywhere,
        scratch_shapes=[pltpu.SemaphoreType.DMA((4,))],
        compiler_params=pltpu.CompilerParams(vmem_limit_bytes=4 * 1024 * 1024),
        name="hand_over",
    )(moved)


def solution(mesh):
    return jax.shard_map(
        body,
        mesh=mesh,
        in_specs=(
            P("dp", "seq", None),
            P("dp", None),
            P("dp", None),
            P(),
            P("dp", "seq"),
            P("dp", "seq"),
            P("dp", "seq"),
            P(),
            P(),
        ),
        out_specs=P("dp", "seq", None),
        check_vma=False,
    )
```

```python
import math

import jax
import jax.numpy as jnp
from jax import lax
from jax.experimental import pallas as pl
from jax.experimental.pallas import tpu as pltpu
from jax.sharding import PartitionSpec as P

EPS = 1e-06
ROPE_BASE = 1000000.0
MESH = pl.DeviceIdType.MESH

SIDE = 4
SEQ = 8
ROWS = 1024
OWN = ROWS // SEQ
PIECE = OWN // 2
TAIL = 16
WIDTH = 5120
SHARD = WIDTH // (SIDE * SIDE)
HALF = SHARD // 2
LINE = SIDE * HALF
LINES = 2 * SIDE
PIECES = LINES * SIDE
HEAD = 128
HEADS = 8
NDOC = 8
WIDE_CHUNKS = 4
NARROW_CHUNKS = 2
CHUNKS = WIDE_CHUNKS + NARROW_CHUNKS
BLK = 16
BLOCKS = ROWS // BLK
QROWS = 256
BAND = 768
MASKED = -1e30
SCALE = math.log2(math.e) / math.sqrt(HEAD)


def place():
    s, d = lax.axis_index("seq"), lax.axis_index("dp")
    return s, d, d // SIDE, d % SIDE


def remote(src, dst, send, recv, seq, dp):
    return pltpu.make_async_remote_copy(
        src_ref=src,
        dst_ref=dst,
        send_sem=send,
        recv_sem=recv,
        device_id={"seq": seq, "dp": dp},
        device_id_type=MESH,
    )


def along(ring, step):
    _, _, x, y = place()
    if ring == 0:
        pos = (x + step + SIDE) % SIDE
        return pos * SIDE + y, pos
    pos = (y + step + SIDE) % SIDE
    return x * SIDE + pos, pos


def chunk(b, j):
    if j < WIDE_CHUNKS:
        return b.wide.at[j]
    return b.wide.at[WIDE_CHUNKS, :, :, pl.ds((j - WIDE_CHUNKS) * HEAD, HEAD)]


def arrived(b, view, sem):
    s, d, _, _ = place()
    remote(view, view, b.context_send, sem, s, d).wait_recv()


def left(b, view, sem):
    s, d, _, _ = place()
    remote(view, view, sem, b.context_recv, s, d).wait_send()


FIRST = ((0, None, 1), (0, None, -1), (-1, 0, 1), (1, 1, -1))
SECOND = ((0, 0, 1), (0, 1, 1), (-1, 0, 1), (0, 1, -1), (0, 0, -1), (1, 1, -1))


def first_send(b, j, kind):
    s, _, x, y = place()
    whose, part, way = FIRST[kind]
    rows = pl.ds(0, HALF) if part is None else pl.ds(part * (HALF // 2), HALF // 2)
    for half in range(2):
        target, _ = along(half, way)
        _, pos = along(half, whose)
        line = half * SIDE + (y if half == 0 else x)
        view = chunk(b, j).at[line * SIDE + pos, rows]
        remote(view, view, b.weight_send.at[j], b.weight_recv.at[j, 0 if kind < 2 else 1], s, target).start()


def second_send(b, j, kind):
    s, _, _, _ = place()
    whose, part, way = SECOND[kind]
    for half in range(2):
        target, _ = along(1 - half, way)
        _, pos = along(1 - half, whose)
        view = chunk(b, j).at[pl.ds((half * SIDE + pos) * SIDE + 2 * part, 2)]
        sem = {0: 2, 3: 2, 1: 3, 4: 3, 2: 4, 5: 4}[kind]
        remote(view, view, b.weight_send.at[j], b.weight_recv.at[j, sem], s, target).start()


def begin_first(b, j):
    for kind in (0, 1):
        first_send(b, j, kind)


def pass_first(b, j):
    arrived(b, chunk(b, j).at[pl.ds(0, 4)], b.weight_recv.at[j, 0])
    for kind in (2, 3):
        first_send(b, j, kind)


def finish_first(b, j):
    arrived(b, chunk(b, j).at[pl.ds(0, 2)], b.weight_recv.at[j, 1])


def begin_second(b, j, part):
    for kind in ((0, 3), (1, 4))[part]:
        second_send(b, j, kind)


def pass_second(b, j):
    arrived(b, chunk(b, j).at[pl.ds(0, 8)], b.weight_recv.at[j, 2])
    for kind in (2, 5):
        second_send(b, j, kind)
    if j + 1 < CHUNKS:
        begin_second(b, j + 1, 1)
    if j + 2 < CHUNKS:
        begin_second(b, j + 2, 0)


def finish_second(b, j, part):
    arrived(b, chunk(b, j).at[pl.ds(0, 8)], b.weight_recv.at[j, 3 + part])


GROUPS = (((0, 3), 0, PIECE), ((1, 4), 0, PIECE), ((2, 5), 0, PIECE - TAIL), ((2, 5), PIECE - TAIL, TAIL))


def rows_of(b, owner, part, group):
    _, start, size = GROUPS[group]
    return b.rows.at[pl.ds(pl.multiple_of(owner * OWN + part * PIECE + start, TAIL), size)]


def row_send(b, kind, group):
    s, d, _, _ = place()
    whose, part, way = SECOND[kind]
    view = rows_of(b, (s + 2 * whose + SEQ) % SEQ, part, group)
    remote(view, view, b.row_send, b.row_recv.at[group], (s + 2 * way + SEQ) % SEQ, d).start()


def rows_arrived(b, group):
    s, d, _, _ = place()
    kinds, _, size = GROUPS[group]
    arrived(b, b.rows.at[pl.ds(0, 2 * size)], b.row_recv.at[group])
    if group == 0:
        for onward in (2, 3):
            for kind in GROUPS[onward][0]:
                row_send(b, kind, onward)
    twin = s + 1 - 2 * (s % 2)
    for kind in kinds:
        whose, part, way = SECOND[kind]
        view = rows_of(b, (s + 2 * (whose - way) + SEQ) % SEQ, part, group)
        remote(view, view, b.twin_send, b.twin_recv.at[group], twin, d).start()


def twin_arrived(b, group):
    size = PIECE if group == len(GROUPS) else GROUPS[group][2]
    arrived(b, b.rows.at[pl.ds(0, 2 * size)], b.twin_recv.at[group])


def begin_rows(b):
    s, d, _, _ = place()
    up, down = (s + 2) % SEQ, (s + SEQ - 2) % SEQ
    for start, target in ((0, up), (PIECE, down), (PIECE // 2, up), (PIECE + PIECE // 2, down)):
        normalize(b, start)
        view = b.rows.at[pl.ds(pl.multiple_of(s * OWN + start, PIECE // 2), PIECE // 2)]
        remote(view, view, b.row_send, b.row_recv.at[0], target, d).start()
    row_send(b, 1, 1)
    row_send(b, 4, 1)
    twin = s + 1 - 2 * (s % 2)
    view = b.rows.at[pl.ds(pl.multiple_of(s * OWN, OWN), OWN)]
    remote(view, view, b.twin_send, b.twin_recv.at[len(GROUPS)], twin, d).start()


def send_context(b, head):
    s, d, _, _ = place()
    columns = pl.ds(pl.multiple_of((s * HEADS + head) * HEAD, HEAD), HEAD)
    for step in range(1, SEQ):
        target = (s + step) % SEQ
        remote(b.send.at[head, target], b.out.at[0, :, columns], b.context_send, b.context_recv, target, d).start()
    pltpu.make_async_copy(b.send.at[head, s], b.out.at[0, :, columns], b.context_own).start()


def finish_context(b):
    arrived(b, b.send.at[:, pl.ds(0, SEQ - 1)], b.context_recv)
    left(b, b.send.at[:, pl.ds(0, SEQ - 1)], b.context_send)
    pltpu.make_async_copy(b.send.at[:, 0], b.send.at[:, 0], b.context_own).wait()


def begin_own(b, j):
    _, _, x, y = place()
    for half in range(2):
        mine = chunk(b, j).at[(half * SIDE + (y if half == 0 else x)) * SIDE + (x if half == 0 else y)]
        if j == 0:
            parts = ((b.key_weight.at[half], mine.at[:, pl.ds(0, HEAD)]), (b.value_weight.at[half], mine.at[:, pl.ds(HEAD, HEAD)]))
        else:
            size = 2 * HEAD if j < WIDE_CHUNKS else HEAD
            start = (j - 1) * 2 * HEAD if j < WIDE_CHUNKS else (WIDE_CHUNKS - 1) * 2 * HEAD + (j - WIDE_CHUNKS) * HEAD
            parts = ((b.w_query.at[half, :, pl.ds(start, size)], mine),)
        for src, dst in parts:
            pltpu.make_async_copy(src, dst, b.own.at[j]).start()


def finish_own(b, j):
    view = chunk(b, j).at[pl.ds(0, 2)]
    pltpu.make_async_copy(view, view, b.own.at[j]).wait()


def normalize(b, start):
    s, _, _, _ = place()

    @pl.loop(start // BLK, (start + PIECE // 2) // BLK)
    def _(i):
        at = pl.multiple_of(i * BLK, BLK)
        wide = b.hidden_here[pl.ds(at, BLK), :].astype(jnp.float32)
        scale = lax.rsqrt(jnp.mean(wide * wide, axis=-1, keepdims=True) + EPS)
        normed = wide * scale * b.input_gain[...]
        parts = [None] * PIECES
        for x in range(SIDE):
            for y in range(SIDE):
                start = (x * SIDE + y) * SHARD
                parts[y * SIDE + x] = normed[:, start : start + HALF]
                parts[(SIDE + x) * SIDE + y] = normed[:, start + HALF : start + SHARD]
        to = pl.multiple_of(s * OWN + at, BLK)
        b.rows[pl.ds(to, BLK), :] = jnp.concatenate(parts, axis=1).astype(jnp.bfloat16)


def tables(b):
    every = b.segments[...].astype(jnp.float32)
    counts = [jnp.sum(jnp.where(every == v, 1.0, 0.0), axis=1, keepdims=True) for v in range(NDOC - 1)]
    lane = lax.broadcasted_iota(jnp.int32, (1, HEAD), 1)
    exponent = (lane % (HEAD // 2)).astype(jnp.float32) * (2.0 / HEAD)
    frequency = jnp.exp(-math.log(ROPE_BASE) * exponent)
    sign = jnp.where(lane < HEAD // 2, -1.0, 1.0)
    down = lax.broadcasted_iota(jnp.int32, (HEAD, HEAD), 0)
    across = lax.broadcasted_iota(jnp.int32, (HEAD, HEAD), 1)
    step = lax.broadcasted_iota(jnp.int32, (HEAD, 1), 0)
    reach = lax.broadcasted_iota(jnp.int32, (HEAD, BAND), 1)

    @pl.loop(0, ROWS // HEAD)
    def _(i):
        at = pl.multiple_of(i * HEAD, HEAD)
        here = b.segments[:, pl.ds(at, HEAD)].astype(jnp.float32)
        column = jnp.sum(jnp.where(down == across, here, 0.0), axis=1, keepdims=True)
        start = jnp.zeros_like(column)
        for v, count in enumerate(counts):
            start = start + jnp.where(column > v, count, 0.0)
        place_of = (step + at).astype(jnp.float32)
        angle = (place_of - start) * frequency
        b.cosine[pl.ds(at, HEAD), :] = jnp.cos(angle)
        b.sine[pl.ds(at, HEAD), :] = jnp.sin(angle) * sign
        key = (reach + ((i // 2) * QROWS + QROWS - BAND)).astype(jnp.float32)
        allowed = (key >= start) & (key <= place_of)
        b.bias[pl.ds(at, HEAD), :] = jnp.where(allowed, 0.0, MASKED)


def turned(b, raw, gain, at):
    scale = lax.rsqrt(jnp.mean(raw * raw, axis=-1, keepdims=True) + EPS)
    normed = raw * scale * gain
    turn = normed * b.cosine[at, :] + pltpu.roll(normed, HEAD // 2, 1) * b.sine[at, :]
    return turn.astype(jnp.bfloat16)


def chip_rows(k):
    s, _, _, _ = place()
    return pl.ds(pl.multiple_of((s // 2 + k) % SIDE * QROWS, QROWS), QROWS)


def project_keys(b, at):
    raw = jnp.dot(b.rows[at, :], b.wide.at[0].reshape(WIDTH, 2 * HEAD)[...], preferred_element_type=jnp.float32)
    b.keys[at, :] = turned(b, raw[:, :HEAD], b.k_gain[...], at)
    b.values[at, :] = raw[:, HEAD:].astype(jnp.bfloat16)


def keep_queries(b, raw, at):
    for h in range(raw.shape[1] // HEAD):
        b.queries[h, at, :] = turned(b, raw[:, h * HEAD : (h + 1) * HEAD], b.q_gain[...], at)


def project_queries(b, j, at):
    raw = jnp.dot(b.rows[at, :], b.wide.at[j].reshape(WIDTH, 2 * HEAD)[...], preferred_element_type=jnp.float32)
    keep_queries(b, raw, at)


FIRST_LINES, NEXT_LINES, LAST_LINES = (0,), (1, 3), (2,)


def lines_product(b, piece, at, steps):
    _, _, x, y = place()
    left_sides, right_sides = [], []
    for half, mine in ((0, y), (1, x)):
        for step in steps:
            line = half * SIDE + (mine + step) % SIDE
            left_sides.append(b.rows[at, pl.ds(pl.multiple_of(line * LINE, HEAD), LINE)])
            right_sides.append(piece[pl.ds(line * SIDE, SIDE)].reshape(LINE, piece.shape[-1]))
    return jnp.dot(
        jnp.concatenate(left_sides, axis=1), jnp.concatenate(right_sides, axis=0), preferred_element_type=jnp.float32
    )


def project_early(b, piece, partial):
    for i in range(ROWS // QROWS):
        at = pl.ds(i * QROWS, QROWS)
        partial[at, :] += lines_product(b, piece, at, NEXT_LINES)


def attend(b, heads, head, query):
    steps = ROWS // QROWS

    def reach_of(i):
        reach = min((i + 1) * QROWS, BAND)
        return reach, pl.ds((i + 1) * QROWS - reach, reach)

    def score(i):
        keys = b.keys[reach_of(i)[1], :]
        return lax.dot_general(query(i), keys, (((1,), (1,)), ((), ())), preferred_element_type=jnp.float32)

    def mix(i, scores):
        reach, keys = reach_of(i)
        bias = b.bias[pl.ds(i * QROWS, QROWS), BAND - reach :]
        weights = jnp.exp2(scores.reshape(heads, QROWS, reach) * SCALE + bias[None]).reshape(heads * QROWS, reach)
        total = jnp.sum(weights, axis=1, keepdims=True)
        mixed = jnp.dot(weights.astype(jnp.bfloat16), b.values[keys, :], preferred_element_type=jnp.float32)
        context = (mixed / total).astype(jnp.bfloat16).reshape(heads, QROWS // BLK, BLK, HEAD)
        for h in range(heads):
            b.context[h, pl.ds(i * (QROWS // BLK), QROWS // BLK)] = context[h]

    scores = score(0)
    for i in range(steps):
        later = score(i + 1) if i + 1 < steps else None
        mix(i, scores)
        scores = later

    per = BLOCKS // SEQ
    for h in range(heads):
        for t in range(SEQ):
            for r in range(per):
                b.send[head + h, t, pl.ds(r * BLK, BLK), :] = b.context[h, b.home[0, t * per + r]]
        send_context(b, head + h)


def attend_kept(b, head, slots):
    def query(i):
        at = pl.ds(i * QROWS, QROWS)
        parts = [b.queries[slot, at, :] for slot in slots]
        return parts[0] if len(parts) == 1 else jnp.concatenate(parts, axis=0)

    attend(b, len(slots), head, query)


def project_late(b, piece, partial):
    for i in range(ROWS // QROWS):
        at = pl.ds(i * QROWS, QROWS)
        keep_queries(b, partial[at, :] + lines_product(b, piece, at, LAST_LINES), at)


def barrier():
    s, d, _, _ = place()
    ready = pltpu.get_barrier_semaphore()
    for ring in range(2):
        for step in (1, -1):
            target, _ = along(ring, step)
            pl.semaphore_signal(ready, inc=1, device_id={"seq": s, "dp": target}, device_id_type=MESH)
    for step in range(1, SEQ):
        pl.semaphore_signal(ready, inc=1, device_id={"seq": (s + step) % SEQ, "dp": d}, device_id_type=MESH)
    pl.semaphore_wait(ready, 4 + SEQ - 1)


class Buffers:
    def __init__(self, names, refs):
        self.__dict__.update(zip(names, refs, strict=True))


SCRATCH = {
    "rows": pltpu.VMEM((ROWS, WIDTH), jnp.bfloat16),
    "wide": pltpu.VMEM((WIDE_CHUNKS + 1, PIECES, HALF, 2 * HEAD), jnp.bfloat16),
    "hidden_here": pltpu.VMEM((OWN, WIDTH), jnp.bfloat16),
    "segments": pltpu.VMEM((1, ROWS), jnp.int32),
    "home": pltpu.SMEM((1, BLOCKS), jnp.int32),
    "input_gain": pltpu.VMEM((1, WIDTH), jnp.float32),
    "q_gain": pltpu.VMEM((1, HEAD), jnp.float32),
    "k_gain": pltpu.VMEM((1, HEAD), jnp.float32),
    "cosine": pltpu.VMEM((ROWS, HEAD), jnp.float32),
    "sine": pltpu.VMEM((ROWS, HEAD), jnp.float32),
    "bias": pltpu.VMEM((ROWS, BAND), jnp.float32),
    "keys": pltpu.VMEM((ROWS, HEAD), jnp.bfloat16),
    "values": pltpu.VMEM((ROWS, HEAD), jnp.bfloat16),
    "queries": pltpu.VMEM((2, ROWS, HEAD), jnp.bfloat16),
    "partial": pltpu.VMEM((WIDE_CHUNKS - 1, ROWS, 2 * HEAD), jnp.float32),
    "context": pltpu.VMEM((2, BLOCKS, BLK, HEAD), jnp.bfloat16),
    "send": pltpu.VMEM((HEADS, SEQ, OWN, HEAD), jnp.bfloat16),
    "small": pltpu.SemaphoreType.DMA((6,)),
    "own": pltpu.SemaphoreType.DMA((CHUNKS,)),
    "weight_send": pltpu.SemaphoreType.DMA((CHUNKS,)),
    "weight_recv": pltpu.SemaphoreType.DMA((CHUNKS, 5)),
    "row_send": pltpu.SemaphoreType.DMA,
    "row_recv": pltpu.SemaphoreType.DMA((len(GROUPS),)),
    "twin_send": pltpu.SemaphoreType.DMA,
    "twin_recv": pltpu.SemaphoreType.DMA((len(GROUPS) + 1,)),
    "context_send": pltpu.SemaphoreType.DMA,
    "context_recv": pltpu.SemaphoreType.DMA,
    "context_own": pltpu.SemaphoreType.DMA,
}
OPERANDS = (
    "hidden",
    "segments_in",
    "home_in",
    "input_gain_in",
    "q_gain_in",
    "k_gain_in",
    "w_query",
    "key_weight",
    "value_weight",
    "out",
)


def kernel(*refs):
    b = Buffers(OPERANDS + tuple(SCRATCH), refs)
    small = [
        pltpu.make_async_copy(src, dst, b.small.at[i])
        for i, (src, dst) in enumerate(
            (
                (b.hidden.at[0], b.hidden_here),
                (b.input_gain_in, b.input_gain),
                (b.segments_in, b.segments),
                (b.home_in, b.home),
                (b.q_gain_in, b.q_gain),
                (b.k_gain_in, b.k_gain),
            )
        )
    ]
    for j in range(CHUNKS):
        begin_own(b, j)
        if j == 0:
            for copy in small:
                copy.start()
    barrier()

    for j in range(2):
        finish_own(b, j)
        begin_first(b, j)
    small[0].wait()
    small[1].wait()
    begin_rows(b)
    for j in range(2, CHUNKS):
        finish_own(b, j)
        begin_first(b, j)
    for copy in small[2:]:
        copy.wait()
    tables(b)
    for j in range(CHUNKS):
        pass_first(b, j)
    finish_first(b, 0)
    begin_second(b, 0, 0)
    begin_second(b, 0, 1)
    finish_first(b, 1)
    begin_second(b, 1, 0)
    for j in range(2, CHUNKS):
        finish_first(b, j)
    rows_arrived(b, 0)
    pass_second(b, 0)
    pass_second(b, 1)
    rows_arrived(b, 1)

    for part in range(2):
        finish_second(b, 0, part)
    for group in (len(GROUPS), 0, 1):
        twin_arrived(b, group)

    @pl.loop(0, SIDE - 1)
    def _(k):
        at = chip_rows((k + 3) % SIDE)
        project_keys(b, at)
        for j in (3, 4):
            b.partial[j - 2, at, :] = lines_product(b, b.wide.at[j], at, FIRST_LINES)

    pass_second(b, 2)
    for part in range(2):
        finish_second(b, 1, part)

    @pl.loop(0, SIDE - 1)
    def _(k):
        project_queries(b, 1, chip_rows((k + 3) % SIDE))

    finish_second(b, 2, 0)

    @pl.loop(0, SIDE - 1)
    def _(k):
        at = chip_rows((k + 3) % SIDE)
        b.partial[0, at, :] = lines_product(b, b.wide.at[2], at, FIRST_LINES + NEXT_LINES)

    for group in (2, 3):
        rows_arrived(b, group)
    for group in (2, 3):
        twin_arrived(b, group)
    project_keys(b, chip_rows(2))
    project_queries(b, 1, chip_rows(2))
    attend_kept(b, 0, (0,))
    attend_kept(b, 1, (1,))

    pass_second(b, 3)
    finish_second(b, 2, 1)
    for k in (3, 0, 1):
        at = chip_rows(k)
        keep_queries(b, b.partial[0, at, :] + lines_product(b, b.wide.at[2], at, LAST_LINES), at)
    project_queries(b, 2, chip_rows(2))
    attend_kept(b, 2, (0, 1))
    for j in (3, 4):
        at = chip_rows(2)
        b.partial[j - 2, at, :] = lines_product(b, b.wide.at[j], at, FIRST_LINES)

    finish_second(b, 3, 0)
    project_early(b, b.wide.at[3], b.partial.at[1])
    pass_second(b, 4)
    finish_second(b, 3, 1)
    project_late(b, b.wide.at[3], b.partial.at[1])
    attend_kept(b, 4, (0, 1))

    for j in range(WIDE_CHUNKS, CHUNKS):
        finish_second(b, j, 0)
        partial = b.partial.at[2, :, pl.ds((j - WIDE_CHUNKS) * HEAD, HEAD)]
        project_early(b, chunk(b, j), partial)
        if j + 1 < CHUNKS:
            pass_second(b, j + 1)
        finish_second(b, j, 1)
        project_late(b, chunk(b, j), partial)
        attend_kept(b, j + 2, (0,))

    for j in range(CHUNKS):
        left(b, chunk(b, j).at[pl.ds(0, PIECES - 2)], b.weight_send.at[j])
    left(b, b.rows.at[pl.ds(0, 6 * PIECE)], b.row_send)
    left(b, b.rows.at[pl.ds(0, OWN + 6 * PIECE)], b.twin_send)
    finish_context(b)


def hand_over(src, dst, sems):
    part = OWN // 4
    copies = [
        pltpu.make_async_copy(src.at[:, pl.ds(i * part, part)], dst.at[:, pl.ds(i * part, part)], sems.at[i])
        for i in range(4)
    ]
    for copy in copies:
        copy.start()
    for copy in copies:
        copy.wait()


def body(hidden_rows, segment_ids, block_home, input_gain, w_query, key_weight, value_weight, q_gain, k_gain):
    anywhere = pl.BlockSpec(memory_space=pl.ANY)
    vector = pl.BlockSpec(memory_space=pltpu.VMEM)
    shape = (1, OWN, SEQ * HEADS * HEAD)
    moved = pl.pallas_call(
        kernel,
        out_shape=pltpu.VMEM(shape, jnp.bfloat16),
        in_specs=[anywhere] * 9,
        out_specs=vector,
        scratch_shapes=list(SCRATCH.values()),
        compiler_params=pltpu.CompilerParams(
            collective_id=0, has_side_effects=True, vmem_limit_bytes=52 * 1024 * 1024
        ),
        name="packed_attention",
    )(
        hidden_rows,
        segment_ids,
        block_home,
        input_gain.reshape(1, WIDTH),
        q_gain.reshape(1, HEAD),
        k_gain.reshape(1, HEAD),
        w_query.reshape(2, HALF, HEADS * HEAD),
        key_weight.reshape(2, HALF, HEAD),
        value_weight.reshape(2, HALF, HEAD),
    )
    return pl.pallas_call(
        hand_over,
        out_shape=jax.ShapeDtypeStruct(shape, jnp.bfloat16),
        in_specs=[vector],
        out_specs=anywhere,
        scratch_shapes=[pltpu.SemaphoreType.DMA((4,))],
        compiler_params=pltpu.CompilerParams(vmem_limit_bytes=4 * 1024 * 1024),
        name="hand_over",
    )(moved)


def solution(mesh):
    return jax.shard_map(
        body,
        mesh=mesh,
        in_specs=(
            P("dp", "seq", None),
            P("dp", None),
            P("dp", None),
            P(),
            P("dp", "seq"),
            P("dp", "seq"),
            P("dp", "seq"),
            P(),
            P(),
        ),
        out_specs=P("dp", "seq", None),
        check_vma=False,
    )
```

```python
import math

import jax
import jax.numpy as jnp
from jax import lax
from jax.experimental import pallas as pl
from jax.experimental.pallas import tpu as pltpu
from jax.sharding import PartitionSpec as P

EPS = 1e-06
ROPE_BASE = 1000000.0
MESH = pl.DeviceIdType.MESH

SIDE = 4
SEQ = 8
ROWS = 1024
OWN = ROWS // SEQ
PIECE = OWN // 2
TAIL = 16
WIDTH = 5120
SHARD = WIDTH // (SIDE * SIDE)
HALF = SHARD // 2
LINE = SIDE * HALF
LINES = 2 * SIDE
PIECES = LINES * SIDE
HEAD = 128
HEADS = 8
NDOC = 8
WIDE_CHUNKS = 4
NARROW_CHUNKS = 2
CHUNKS = WIDE_CHUNKS + NARROW_CHUNKS
BLK = 16
BLOCKS = ROWS // BLK
QROWS = 256
BAND = 768
MASKED = -1e30
SCALE = math.log2(math.e) / math.sqrt(HEAD)


def place():
    s, d = lax.axis_index("seq"), lax.axis_index("dp")
    return s, d, d // SIDE, d % SIDE


def remote(src, dst, send, recv, seq, dp):
    return pltpu.make_async_remote_copy(
        src_ref=src,
        dst_ref=dst,
        send_sem=send,
        recv_sem=recv,
        device_id={"seq": seq, "dp": dp},
        device_id_type=MESH,
    )


def along(ring, step):
    _, _, x, y = place()
    if ring == 0:
        pos = (x + step + SIDE) % SIDE
        return pos * SIDE + y, pos
    pos = (y + step + SIDE) % SIDE
    return x * SIDE + pos, pos


def chunk(b, j):
    if j < WIDE_CHUNKS:
        return b.wide.at[j]
    return b.wide.at[WIDE_CHUNKS, :, :, pl.ds((j - WIDE_CHUNKS) * HEAD, HEAD)]


def arrived(b, view, sem):
    s, d, _, _ = place()
    remote(view, view, b.context_send, sem, s, d).wait_recv()


def left(b, view, sem):
    s, d, _, _ = place()
    remote(view, view, sem, b.context_recv, s, d).wait_send()


FIRST = ((0, None, 1), (0, None, -1), (-1, 0, 1), (1, 1, -1))
SECOND = ((0, 0, 1), (0, 1, 1), (-1, 0, 1), (0, 1, -1), (0, 0, -1), (1, 1, -1))


def first_send(b, j, kind):
    s, _, x, y = place()
    whose, part, way = FIRST[kind]
    rows = pl.ds(0, HALF) if part is None else pl.ds(part * (HALF // 2), HALF // 2)
    for half in range(2):
        target, _ = along(half, way)
        _, pos = along(half, whose)
        line = half * SIDE + (y if half == 0 else x)
        view = chunk(b, j).at[line * SIDE + pos, rows]
        remote(view, view, b.weight_send.at[j], b.weight_recv.at[j, 0 if kind < 2 else 1], s, target).start()


def second_send(b, j, kind):
    s, _, _, _ = place()
    whose, part, way = SECOND[kind]
    for half in range(2):
        target, _ = along(1 - half, way)
        _, pos = along(1 - half, whose)
        view = chunk(b, j).at[pl.ds((half * SIDE + pos) * SIDE + 2 * part, 2)]
        sem = {0: 2, 3: 2, 1: 3, 4: 3, 2: 4, 5: 4}[kind]
        remote(view, view, b.weight_send.at[j], b.weight_recv.at[j, sem], s, target).start()


def begin_first(b, j):
    for kind in (0, 1):
        first_send(b, j, kind)


def pass_first(b, j):
    arrived(b, chunk(b, j).at[pl.ds(0, 4)], b.weight_recv.at[j, 0])
    for kind in (2, 3):
        first_send(b, j, kind)


def finish_first(b, j):
    arrived(b, chunk(b, j).at[pl.ds(0, 2)], b.weight_recv.at[j, 1])


def begin_second(b, j, part):
    for kind in ((0, 3), (1, 4))[part]:
        second_send(b, j, kind)


def pass_second(b, j):
    arrived(b, chunk(b, j).at[pl.ds(0, 8)], b.weight_recv.at[j, 2])
    for kind in (2, 5):
        second_send(b, j, kind)
    if j + 1 < CHUNKS:
        begin_second(b, j + 1, 1)
    if j + 2 < CHUNKS:
        begin_second(b, j + 2, 0)


def finish_second(b, j, part):
    arrived(b, chunk(b, j).at[pl.ds(0, 8)], b.weight_recv.at[j, 3 + part])


GROUPS = (((0, 3), 0, PIECE), ((1, 4), 0, PIECE), ((2, 5), 0, PIECE - TAIL), ((2, 5), PIECE - TAIL, TAIL))


def rows_of(b, owner, part, group):
    _, start, size = GROUPS[group]
    return b.rows.at[pl.ds(pl.multiple_of(owner * OWN + part * PIECE + start, TAIL), size)]


def row_send(b, kind, group):
    s, d, _, _ = place()
    whose, part, way = SECOND[kind]
    view = rows_of(b, (s + 2 * whose + SEQ) % SEQ, part, group)
    remote(view, view, b.row_send, b.row_recv.at[group], (s + 2 * way + SEQ) % SEQ, d).start()


def rows_arrived(b, group):
    s, d, _, _ = place()
    kinds, _, size = GROUPS[group]
    arrived(b, b.rows.at[pl.ds(0, 2 * size)], b.row_recv.at[group])
    if group == 0:
        for onward in (2, 3):
            for kind in GROUPS[onward][0]:
                row_send(b, kind, onward)
    twin = s + 1 - 2 * (s % 2)
    for kind in kinds:
        whose, part, way = SECOND[kind]
        view = rows_of(b, (s + 2 * (whose - way) + SEQ) % SEQ, part, group)
        remote(view, view, b.twin_send, b.twin_recv.at[group], twin, d).start()


def twin_arrived(b, group):
    size = PIECE if group == len(GROUPS) else GROUPS[group][2]
    arrived(b, b.rows.at[pl.ds(0, 2 * size)], b.twin_recv.at[group])


def begin_rows(b):
    s, d, _, _ = place()
    up, down = (s + 2) % SEQ, (s + SEQ - 2) % SEQ
    for start, target in ((0, up), (PIECE, down), (PIECE // 2, up), (PIECE + PIECE // 2, down)):
        normalize(b, start)
        view = b.rows.at[pl.ds(pl.multiple_of(s * OWN + start, PIECE // 2), PIECE // 2)]
        remote(view, view, b.row_send, b.row_recv.at[0], target, d).start()
    row_send(b, 1, 1)
    row_send(b, 4, 1)
    twin = s + 1 - 2 * (s % 2)
    view = b.rows.at[pl.ds(pl.multiple_of(s * OWN, OWN), OWN)]
    remote(view, view, b.twin_send, b.twin_recv.at[len(GROUPS)], twin, d).start()


def send_context(b, head):
    s, d, _, _ = place()
    columns = pl.ds(pl.multiple_of((s * HEADS + head) * HEAD, HEAD), HEAD)
    for step in range(1, SEQ):
        target = (s + step) % SEQ
        remote(b.send.at[head, target], b.out.at[0, :, columns], b.context_send, b.context_recv, target, d).start()
    pltpu.make_async_copy(b.send.at[head, s], b.out.at[0, :, columns], b.context_own).start()


def finish_context(b):
    arrived(b, b.send.at[:, pl.ds(0, SEQ - 1)], b.context_recv)
    left(b, b.send.at[:, pl.ds(0, SEQ - 1)], b.context_send)
    pltpu.make_async_copy(b.send.at[:, 0], b.send.at[:, 0], b.context_own).wait()


def begin_own(b, j):
    _, _, x, y = place()
    for half in range(2):
        mine = chunk(b, j).at[(half * SIDE + (y if half == 0 else x)) * SIDE + (x if half == 0 else y)]
        if j == 0:
            parts = ((b.key_weight.at[half], mine.at[:, pl.ds(0, HEAD)]), (b.value_weight.at[half], mine.at[:, pl.ds(HEAD, HEAD)]))
        else:
            size = 2 * HEAD if j < WIDE_CHUNKS else HEAD
            start = (j - 1) * 2 * HEAD if j < WIDE_CHUNKS else (WIDE_CHUNKS - 1) * 2 * HEAD + (j - WIDE_CHUNKS) * HEAD
            parts = ((b.w_query.at[half, :, pl.ds(start, size)], mine),)
        for src, dst in parts:
            pltpu.make_async_copy(src, dst, b.own.at[j]).start()


def finish_own(b, j):
    view = chunk(b, j).at[pl.ds(0, 2)]
    pltpu.make_async_copy(view, view, b.own.at[j]).wait()


def normalize(b, start):
    s, _, _, _ = place()

    @pl.loop(start // BLK, (start + PIECE // 2) // BLK)
    def _(i):
        at = pl.multiple_of(i * BLK, BLK)
        wide = b.hidden_here[pl.ds(at, BLK), :].astype(jnp.float32)
        scale = lax.rsqrt(jnp.mean(wide * wide, axis=-1, keepdims=True) + EPS)
        normed = wide * scale * b.input_gain[...]
        parts = [None] * PIECES
        for x in range(SIDE):
            for y in range(SIDE):
                start = (x * SIDE + y) * SHARD
                parts[y * SIDE + x] = normed[:, start : start + HALF]
                parts[(SIDE + x) * SIDE + y] = normed[:, start + HALF : start + SHARD]
        to = pl.multiple_of(s * OWN + at, BLK)
        b.rows[pl.ds(to, BLK), :] = jnp.concatenate(parts, axis=1).astype(jnp.bfloat16)


def tables(b):
    every = b.segments[...].astype(jnp.float32)
    counts = [jnp.sum(jnp.where(every == v, 1.0, 0.0), axis=1, keepdims=True) for v in range(NDOC - 1)]
    lane = lax.broadcasted_iota(jnp.int32, (1, HEAD), 1)
    exponent = (lane % (HEAD // 2)).astype(jnp.float32) * (2.0 / HEAD)
    frequency = jnp.exp(-math.log(ROPE_BASE) * exponent)
    sign = jnp.where(lane < HEAD // 2, -1.0, 1.0)
    down = lax.broadcasted_iota(jnp.int32, (HEAD, HEAD), 0)
    across = lax.broadcasted_iota(jnp.int32, (HEAD, HEAD), 1)
    step = lax.broadcasted_iota(jnp.int32, (HEAD, 1), 0)
    reach = lax.broadcasted_iota(jnp.int32, (HEAD, BAND), 1)

    @pl.loop(0, ROWS // HEAD)
    def _(i):
        at = pl.multiple_of(i * HEAD, HEAD)
        here = b.segments[:, pl.ds(at, HEAD)].astype(jnp.float32)
        column = jnp.sum(jnp.where(down == across, here, 0.0), axis=1, keepdims=True)
        start = jnp.zeros_like(column)
        for v, count in enumerate(counts):
            start = start + jnp.where(column > v, count, 0.0)
        place_of = (step + at).astype(jnp.float32)
        angle = (place_of - start) * frequency
        b.cosine[pl.ds(at, HEAD), :] = jnp.cos(angle)
        b.sine[pl.ds(at, HEAD), :] = jnp.sin(angle) * sign
        key = (reach + ((i // 2) * QROWS + QROWS - BAND)).astype(jnp.float32)
        allowed = (key >= start) & (key <= place_of)
        b.bias[pl.ds(at, HEAD), :] = jnp.where(allowed, 0.0, MASKED)


def turned(b, raw, gain, at):
    scale = lax.rsqrt(jnp.mean(raw * raw, axis=-1, keepdims=True) + EPS)
    normed = raw * scale * gain
    turn = normed * b.cosine[at, :] + pltpu.roll(normed, HEAD // 2, 1) * b.sine[at, :]
    return turn.astype(jnp.bfloat16)


def chip_rows(k):
    s, _, _, _ = place()
    return pl.ds(pl.multiple_of((s // 2 + k) % SIDE * QROWS, QROWS), QROWS)


def project_keys(b, at):
    raw = jnp.dot(b.rows[at, :], b.wide.at[0].reshape(WIDTH, 2 * HEAD)[...], preferred_element_type=jnp.float32)
    b.keys[at, :] = turned(b, raw[:, :HEAD], b.k_gain[...], at)
    b.values[at, :] = raw[:, HEAD:].astype(jnp.bfloat16)


def keep_queries(b, raw, at):
    for h in range(raw.shape[1] // HEAD):
        b.queries[h, at, :] = turned(b, raw[:, h * HEAD : (h + 1) * HEAD], b.q_gain[...], at)


def project_queries(b, j, at):
    raw = jnp.dot(b.rows[at, :], b.wide.at[j].reshape(WIDTH, 2 * HEAD)[...], preferred_element_type=jnp.float32)
    keep_queries(b, raw, at)


FIRST_LINES, NEXT_LINES, LAST_LINES = (0,), (1, 3), (2,)


def lines_product(b, piece, at, steps):
    _, _, x, y = place()
    left_sides, right_sides = [], []
    for half, mine in ((0, y), (1, x)):
        for step in steps:
            line = half * SIDE + (mine + step) % SIDE
            left_sides.append(b.rows[at, pl.ds(pl.multiple_of(line * LINE, HEAD), LINE)])
            right_sides.append(piece[pl.ds(line * SIDE, SIDE)].reshape(LINE, piece.shape[-1]))
    return jnp.dot(
        jnp.concatenate(left_sides, axis=1), jnp.concatenate(right_sides, axis=0), preferred_element_type=jnp.float32
    )


def project_early(b, piece, partial):
    for i in range(ROWS // QROWS):
        at = pl.ds(i * QROWS, QROWS)
        partial[at, :] += lines_product(b, piece, at, NEXT_LINES)


def attend(b, heads, head, query):
    steps = ROWS // QROWS

    def reach_of(i):
        reach = min((i + 1) * QROWS, BAND)
        return reach, pl.ds((i + 1) * QROWS - reach, reach)

    def score(i):
        keys = b.keys[reach_of(i)[1], :]
        return lax.dot_general(query(i), keys, (((1,), (1,)), ((), ())), preferred_element_type=jnp.float32)

    def mix(i, scores):
        reach, keys = reach_of(i)
        bias = b.bias[pl.ds(i * QROWS, QROWS), BAND - reach :]
        weights = jnp.exp2(scores.reshape(heads, QROWS, reach) * SCALE + bias[None]).reshape(heads * QROWS, reach)
        total = jnp.sum(weights, axis=1, keepdims=True)
        mixed = jnp.dot(weights.astype(jnp.bfloat16), b.values[keys, :], preferred_element_type=jnp.float32)
        context = (mixed / total).astype(jnp.bfloat16).reshape(heads, QROWS // BLK, BLK, HEAD)
        for h in range(heads):
            b.context[h, pl.ds(i * (QROWS // BLK), QROWS // BLK)] = context[h]

    scores = score(0)
    for i in range(steps):
        later = score(i + 1) if i + 1 < steps else None
        mix(i, scores)
        scores = later

    per = BLOCKS // SEQ
    for h in range(heads):
        for t in range(SEQ):
            for r in range(per):
                b.send[head + h, t, pl.ds(r * BLK, BLK), :] = b.context[h, b.home[0, t * per + r]]
        send_context(b, head + h)


def attend_kept(b, head, slots):
    def query(i):
        at = pl.ds(i * QROWS, QROWS)
        parts = [b.queries[slot, at, :] for slot in slots]
        return parts[0] if len(parts) == 1 else jnp.concatenate(parts, axis=0)

    attend(b, len(slots), head, query)


def project_late(b, piece, partial):
    for i in range(ROWS // QROWS):
        at = pl.ds(i * QROWS, QROWS)
        keep_queries(b, partial[at, :] + lines_product(b, piece, at, LAST_LINES), at)


def barrier():
    s, d, _, _ = place()
    ready = pltpu.get_barrier_semaphore()
    for ring in range(2):
        for step in (1, -1):
            target, _ = along(ring, step)
            pl.semaphore_signal(ready, inc=1, device_id={"seq": s, "dp": target}, device_id_type=MESH)
    for step in range(1, SEQ):
        pl.semaphore_signal(ready, inc=1, device_id={"seq": (s + step) % SEQ, "dp": d}, device_id_type=MESH)
    pl.semaphore_wait(ready, 4 + SEQ - 1)


class Buffers:
    def __init__(self, names, refs):
        self.__dict__.update(zip(names, refs, strict=True))


SCRATCH = {
    "rows": pltpu.VMEM((ROWS, WIDTH), jnp.bfloat16),
    "wide": pltpu.VMEM((WIDE_CHUNKS + 1, PIECES, HALF, 2 * HEAD), jnp.bfloat16),
    "hidden_here": pltpu.VMEM((OWN, WIDTH), jnp.bfloat16),
    "segments": pltpu.VMEM((1, ROWS), jnp.int32),
    "home": pltpu.SMEM((1, BLOCKS), jnp.int32),
    "input_gain": pltpu.VMEM((1, WIDTH), jnp.float32),
    "q_gain": pltpu.VMEM((1, HEAD), jnp.float32),
    "k_gain": pltpu.VMEM((1, HEAD), jnp.float32),
    "cosine": pltpu.VMEM((ROWS, HEAD), jnp.float32),
    "sine": pltpu.VMEM((ROWS, HEAD), jnp.float32),
    "bias": pltpu.VMEM((ROWS, BAND), jnp.float32),
    "keys": pltpu.VMEM((ROWS, HEAD), jnp.bfloat16),
    "values": pltpu.VMEM((ROWS, HEAD), jnp.bfloat16),
    "queries": pltpu.VMEM((2, ROWS, HEAD), jnp.bfloat16),
    "partial": pltpu.VMEM((WIDE_CHUNKS - 1, ROWS, 2 * HEAD), jnp.float32),
    "context": pltpu.VMEM((2, BLOCKS, BLK, HEAD), jnp.bfloat16),
    "send": pltpu.VMEM((HEADS, SEQ, OWN, HEAD), jnp.bfloat16),
    "small": pltpu.SemaphoreType.DMA((6,)),
    "own": pltpu.SemaphoreType.DMA((CHUNKS,)),
    "weight_send": pltpu.SemaphoreType.DMA((CHUNKS,)),
    "weight_recv": pltpu.SemaphoreType.DMA((CHUNKS, 5)),
    "row_send": pltpu.SemaphoreType.DMA,
    "row_recv": pltpu.SemaphoreType.DMA((len(GROUPS),)),
    "twin_send": pltpu.SemaphoreType.DMA,
    "twin_recv": pltpu.SemaphoreType.DMA((len(GROUPS) + 1,)),
    "context_send": pltpu.SemaphoreType.DMA,
    "context_recv": pltpu.SemaphoreType.DMA,
    "context_own": pltpu.SemaphoreType.DMA,
}
OPERANDS = (
    "hidden",
    "segments_in",
    "home_in",
    "input_gain_in",
    "q_gain_in",
    "k_gain_in",
    "w_query",
    "key_weight",
    "value_weight",
    "out",
)


def kernel(*refs):
    b = Buffers(OPERANDS + tuple(SCRATCH), refs)
    small = [
        pltpu.make_async_copy(src, dst, b.small.at[i])
        for i, (src, dst) in enumerate(
            (
                (b.hidden.at[0], b.hidden_here),
                (b.input_gain_in, b.input_gain),
                (b.segments_in, b.segments),
                (b.home_in, b.home),
                (b.q_gain_in, b.q_gain),
                (b.k_gain_in, b.k_gain),
            )
        )
    ]
    for j in range(CHUNKS):
        begin_own(b, j)
        if j == 0:
            for copy in small:
                copy.start()
    barrier()

    for j in range(2):
        finish_own(b, j)
        begin_first(b, j)
    small[0].wait()
    small[1].wait()
    begin_rows(b)
    for j in range(2, CHUNKS):
        finish_own(b, j)
        begin_first(b, j)
    for copy in small[2:]:
        copy.wait()
    tables(b)
    for j in range(CHUNKS):
        pass_first(b, j)
    finish_first(b, 0)
    begin_second(b, 0, 0)
    begin_second(b, 0, 1)
    finish_first(b, 1)
    begin_second(b, 1, 0)
    for j in range(2, CHUNKS):
        finish_first(b, j)
    rows_arrived(b, 0)
    pass_second(b, 0)
    pass_second(b, 1)
    rows_arrived(b, 1)

    for part in range(2):
        finish_second(b, 0, part)
    for group in (len(GROUPS), 0, 1):
        twin_arrived(b, group)

    @pl.loop(0, SIDE - 1)
    def _(k):
        at = chip_rows((k + 3) % SIDE)
        project_keys(b, at)
        for j in (3, 4):
            b.partial[j - 2, at, :] = lines_product(b, b.wide.at[j], at, FIRST_LINES)

    pass_second(b, 2)
    for part in range(2):
        finish_second(b, 1, part)

    @pl.loop(0, SIDE - 1)
    def _(k):
        project_queries(b, 1, chip_rows((k + 3) % SIDE))

    finish_second(b, 2, 0)

    @pl.loop(0, SIDE - 1)
    def _(k):
        at = chip_rows((k + 3) % SIDE)
        b.partial[0, at, :] = lines_product(b, b.wide.at[2], at, FIRST_LINES + NEXT_LINES)

    for group in (2, 3):
        rows_arrived(b, group)
    for group in (2, 3):
        twin_arrived(b, group)
    project_keys(b, chip_rows(2))
    project_queries(b, 1, chip_rows(2))

    @pl.loop(0, 2)
    def _(h):
        attend_kept(b, h, (h,))

    pass_second(b, 3)
    finish_second(b, 2, 1)
    for k in (3, 0, 1):
        at = chip_rows(k)
        keep_queries(b, b.partial[0, at, :] + lines_product(b, b.wide.at[2], at, LAST_LINES), at)
    project_queries(b, 2, chip_rows(2))
    attend_kept(b, 2, (0, 1))
    for j in (3, 4):
        at = chip_rows(2)
        b.partial[j - 2, at, :] = lines_product(b, b.wide.at[j], at, FIRST_LINES)

    finish_second(b, 3, 0)
    project_early(b, b.wide.at[3], b.partial.at[1])
    pass_second(b, 4)
    finish_second(b, 3, 1)
    project_late(b, b.wide.at[3], b.partial.at[1])
    attend_kept(b, 4, (0, 1))

    @pl.loop(0, NARROW_CHUNKS)
    def _(n):
        columns = pl.ds(pl.multiple_of(n * HEAD, HEAD), HEAD)
        piece, partial = b.wide.at[WIDE_CHUNKS, :, :, columns], b.partial.at[2, :, columns]
        arrived(b, b.wide.at[WIDE_CHUNKS, pl.ds(0, 4)], b.weight_recv.at[WIDE_CHUNKS + n, 3])
        project_early(b, piece, partial)

        @pl.when(n == 0)
        def _():
            pass_second(b, CHUNKS - 1)

        arrived(b, b.wide.at[WIDE_CHUNKS, pl.ds(0, 4)], b.weight_recv.at[WIDE_CHUNKS + n, 4])
        project_late(b, piece, partial)
        attend_kept(b, 2 * (WIDE_CHUNKS - 1) + n, (0,))

    for j in range(CHUNKS):
        left(b, chunk(b, j).at[pl.ds(0, PIECES - 2)], b.weight_send.at[j])
    left(b, b.rows.at[pl.ds(0, 6 * PIECE)], b.row_send)
    left(b, b.rows.at[pl.ds(0, OWN + 6 * PIECE)], b.twin_send)
    finish_context(b)


def hand_over(src, dst, sems):
    part = OWN // 4
    copies = [
        pltpu.make_async_copy(src.at[:, pl.ds(i * part, part)], dst.at[:, pl.ds(i * part, part)], sems.at[i])
        for i in range(4)
    ]
    for copy in copies:
        copy.start()
    for copy in copies:
        copy.wait()


def body(hidden_rows, segment_ids, block_home, input_gain, w_query, key_weight, value_weight, q_gain, k_gain):
    anywhere = pl.BlockSpec(memory_space=pl.ANY)
    vector = pl.BlockSpec(memory_space=pltpu.VMEM)
    shape = (1, OWN, SEQ * HEADS * HEAD)
    moved = pl.pallas_call(
        kernel,
        out_shape=pltpu.VMEM(shape, jnp.bfloat16),
        in_specs=[anywhere] * 9,
        out_specs=vector,
        scratch_shapes=list(SCRATCH.values()),
        compiler_params=pltpu.CompilerParams(
            collective_id=0, has_side_effects=True, vmem_limit_bytes=52 * 1024 * 1024
        ),
        name="packed_attention",
    )(
        hidden_rows,
        segment_ids,
        block_home,
        input_gain.reshape(1, WIDTH),
        q_gain.reshape(1, HEAD),
        k_gain.reshape(1, HEAD),
        w_query.reshape(2, HALF, HEADS * HEAD),
        key_weight.reshape(2, HALF, HEAD),
        value_weight.reshape(2, HALF, HEAD),
    )
    return pl.pallas_call(
        hand_over,
        out_shape=jax.ShapeDtypeStruct(shape, jnp.bfloat16),
        in_specs=[vector],
        out_specs=anywhere,
        scratch_shapes=[pltpu.SemaphoreType.DMA((4,))],
        compiler_params=pltpu.CompilerParams(vmem_limit_bytes=4 * 1024 * 1024),
        name="hand_over",
    )(moved)


def solution(mesh):
    return jax.shard_map(
        body,
        mesh=mesh,
        in_specs=(
            P("dp", "seq", None),
            P("dp", None),
            P("dp", None),
            P(),
            P("dp", "seq"),
            P("dp", "seq"),
            P("dp", "seq"),
            P(),
            P(),
        ),
        out_specs=P("dp", "seq", None),
        check_vma=False,
    )
```

```python
import math

import jax
import jax.numpy as jnp
from jax import lax
from jax.experimental import pallas as pl
from jax.experimental.pallas import tpu as pltpu
from jax.sharding import PartitionSpec as P

EPS = 1e-06
ROPE_BASE = 1000000.0
MESH = pl.DeviceIdType.MESH

SIDE = 4
SEQ = 8
ROWS = 1024
OWN = ROWS // SEQ
PIECE = OWN // 2
TAIL = 16
WIDTH = 5120
SHARD = WIDTH // (SIDE * SIDE)
HALF = SHARD // 2
LINE = SIDE * HALF
LINES = 2 * SIDE
PIECES = LINES * SIDE
HEAD = 128
HEADS = 8
NDOC = 8
WIDE_CHUNKS = 4
NARROW_CHUNKS = 2
CHUNKS = WIDE_CHUNKS + NARROW_CHUNKS
BLK = 16
BLOCKS = ROWS // BLK
QROWS = 256
BAND = 768
MASKED = -1e30
SCALE = math.log2(math.e) / math.sqrt(HEAD)


def place():
    s, d = lax.axis_index("seq"), lax.axis_index("dp")
    return s, d, d // SIDE, d % SIDE


def remote(src, dst, send, recv, seq, dp):
    return pltpu.make_async_remote_copy(
        src_ref=src,
        dst_ref=dst,
        send_sem=send,
        recv_sem=recv,
        device_id={"seq": seq, "dp": dp},
        device_id_type=MESH,
    )


def along(ring, step):
    _, _, x, y = place()
    if ring == 0:
        pos = (x + step + SIDE) % SIDE
        return pos * SIDE + y, pos
    pos = (y + step + SIDE) % SIDE
    return x * SIDE + pos, pos


def chunk(b, j):
    if j < WIDE_CHUNKS:
        return b.wide.at[j]
    return b.wide.at[WIDE_CHUNKS, :, :, pl.ds((j - WIDE_CHUNKS) * HEAD, HEAD)]


def arrived(b, view, sem):
    s, d, _, _ = place()
    remote(view, view, b.context_send, sem, s, d).wait_recv()


def left(b, view, sem):
    s, d, _, _ = place()
    remote(view, view, sem, b.context_recv, s, d).wait_send()


FIRST = ((0, None, 1), (0, None, -1), (-1, 0, 1), (1, 1, -1))
SECOND = ((0, 0, 1), (0, 1, 1), (-1, 0, 1), (0, 1, -1), (0, 0, -1), (1, 1, -1))


def first_send(b, j, kind):
    s, _, x, y = place()
    whose, part, way = FIRST[kind]
    rows = pl.ds(0, HALF) if part is None else pl.ds(part * (HALF // 2), HALF // 2)
    for half in range(2):
        target, _ = along(half, way)
        _, pos = along(half, whose)
        line = half * SIDE + (y if half == 0 else x)
        view = chunk(b, j).at[line * SIDE + pos, rows]
        remote(view, view, b.weight_send.at[j], b.weight_recv.at[j, 0 if kind < 2 else 1], s, target).start()


def second_send(b, j, kind):
    s, _, _, _ = place()
    whose, part, way = SECOND[kind]
    for half in range(2):
        target, _ = along(1 - half, way)
        _, pos = along(1 - half, whose)
        view = chunk(b, j).at[pl.ds((half * SIDE + pos) * SIDE + 2 * part, 2)]
        sem = {0: 2, 3: 2, 1: 3, 4: 3, 2: 4, 5: 4}[kind]
        remote(view, view, b.weight_send.at[j], b.weight_recv.at[j, sem], s, target).start()


def begin_first(b, j):
    for kind in (0, 1):
        first_send(b, j, kind)


def pass_first(b, j):
    arrived(b, chunk(b, j).at[pl.ds(0, 4)], b.weight_recv.at[j, 0])
    for kind in (2, 3):
        first_send(b, j, kind)


def finish_first(b, j):
    arrived(b, chunk(b, j).at[pl.ds(0, 2)], b.weight_recv.at[j, 1])


def begin_second(b, j, part):
    for kind in ((0, 3), (1, 4))[part]:
        second_send(b, j, kind)


QUEUE = (((1, 1), (2, 0)), ((2, 1), (3, 0)), ((3, 1),), ((4, 0), (4, 1), (5, 0)), ((5, 1),), ())


def pass_second(b, j):
    arrived(b, chunk(b, j).at[pl.ds(0, 8)], b.weight_recv.at[j, 2])
    for kind in (2, 5):
        second_send(b, j, kind)
    for other, part in QUEUE[j]:
        begin_second(b, other, part)


def finish_second(b, j, part):
    arrived(b, chunk(b, j).at[pl.ds(0, 8)], b.weight_recv.at[j, 3 + part])


GROUPS = (((0, 3), 0, PIECE), ((1, 4), 0, PIECE), ((2, 5), 0, PIECE - TAIL), ((2, 5), PIECE - TAIL, TAIL))


def rows_of(b, owner, part, group):
    _, start, size = GROUPS[group]
    return b.rows.at[pl.ds(pl.multiple_of(owner * OWN + part * PIECE + start, TAIL), size)]


def row_send(b, kind, group):
    s, d, _, _ = place()
    whose, part, way = SECOND[kind]
    view = rows_of(b, (s + 2 * whose + SEQ) % SEQ, part, group)
    remote(view, view, b.row_send, b.row_recv.at[group], (s + 2 * way + SEQ) % SEQ, d).start()


def rows_arrived(b, group):
    s, d, _, _ = place()
    kinds, _, size = GROUPS[group]
    arrived(b, b.rows.at[pl.ds(0, 2 * size)], b.row_recv.at[group])
    if group == 0:
        for onward in (2, 3):
            for kind in GROUPS[onward][0]:
                row_send(b, kind, onward)
    twin = s + 1 - 2 * (s % 2)
    for kind in kinds:
        whose, part, way = SECOND[kind]
        view = rows_of(b, (s + 2 * (whose - way) + SEQ) % SEQ, part, group)
        remote(view, view, b.twin_send, b.twin_recv.at[group], twin, d).start()


def twin_arrived(b, group):
    size = PIECE if group == len(GROUPS) else GROUPS[group][2]
    arrived(b, b.rows.at[pl.ds(0, 2 * size)], b.twin_recv.at[group])


def begin_rows(b):
    s, d, _, _ = place()
    up, down = (s + 2) % SEQ, (s + SEQ - 2) % SEQ
    for start, target in ((0, up), (PIECE, down), (PIECE // 2, up), (PIECE + PIECE // 2, down)):
        normalize(b, start)
        view = b.rows.at[pl.ds(pl.multiple_of(s * OWN + start, PIECE // 2), PIECE // 2)]
        remote(view, view, b.row_send, b.row_recv.at[0], target, d).start()
    row_send(b, 1, 1)
    row_send(b, 4, 1)
    twin = s + 1 - 2 * (s % 2)
    view = b.rows.at[pl.ds(pl.multiple_of(s * OWN, OWN), OWN)]
    remote(view, view, b.twin_send, b.twin_recv.at[len(GROUPS)], twin, d).start()


def send_context(b, head):
    s, d, _, _ = place()
    columns = pl.ds(pl.multiple_of((s * HEADS + head) * HEAD, HEAD), HEAD)
    for step in range(1, SEQ):
        target = (s + step) % SEQ
        remote(b.send.at[head, target], b.out.at[0, :, columns], b.context_send, b.context_recv, target, d).start()
    pltpu.make_async_copy(b.send.at[head, s], b.out.at[0, :, columns], b.context_own).start()


def finish_context(b):
    arrived(b, b.send.at[:, pl.ds(0, SEQ - 1)], b.context_recv)
    left(b, b.send.at[:, pl.ds(0, SEQ - 1)], b.context_send)
    pltpu.make_async_copy(b.send.at[:, 0], b.send.at[:, 0], b.context_own).wait()


def begin_own(b, j):
    _, _, x, y = place()
    for half in range(2):
        mine = chunk(b, j).at[(half * SIDE + (y if half == 0 else x)) * SIDE + (x if half == 0 else y)]
        if j == 0:
            parts = ((b.key_weight.at[half], mine.at[:, pl.ds(0, HEAD)]), (b.value_weight.at[half], mine.at[:, pl.ds(HEAD, HEAD)]))
        else:
            size = 2 * HEAD if j < WIDE_CHUNKS else HEAD
            start = (j - 1) * 2 * HEAD if j < WIDE_CHUNKS else (WIDE_CHUNKS - 1) * 2 * HEAD + (j - WIDE_CHUNKS) * HEAD
            parts = ((b.w_query.at[half, :, pl.ds(start, size)], mine),)
        for src, dst in parts:
            pltpu.make_async_copy(src, dst, b.own.at[j]).start()


def finish_own(b, j):
    view = chunk(b, j).at[pl.ds(0, 2)]
    pltpu.make_async_copy(view, view, b.own.at[j]).wait()


def normalize(b, start):
    s, _, _, _ = place()

    @pl.loop(start // BLK, (start + PIECE // 2) // BLK)
    def _(i):
        at = pl.multiple_of(i * BLK, BLK)
        wide = b.hidden_here[pl.ds(at, BLK), :].astype(jnp.float32)
        scale = lax.rsqrt(jnp.mean(wide * wide, axis=-1, keepdims=True) + EPS)
        normed = wide * scale * b.input_gain[...]
        parts = [None] * PIECES
        for x in range(SIDE):
            for y in range(SIDE):
                start = (x * SIDE + y) * SHARD
                parts[y * SIDE + x] = normed[:, start : start + HALF]
                parts[(SIDE + x) * SIDE + y] = normed[:, start + HALF : start + SHARD]
        to = pl.multiple_of(s * OWN + at, BLK)
        b.rows[pl.ds(to, BLK), :] = jnp.concatenate(parts, axis=1).astype(jnp.bfloat16)


def tables(b):
    every = b.segments[...].astype(jnp.float32)
    counts = [jnp.sum(jnp.where(every == v, 1.0, 0.0), axis=1, keepdims=True) for v in range(NDOC - 1)]
    lane = lax.broadcasted_iota(jnp.int32, (1, HEAD), 1)
    exponent = (lane % (HEAD // 2)).astype(jnp.float32) * (2.0 / HEAD)
    frequency = jnp.exp(-math.log(ROPE_BASE) * exponent)
    sign = jnp.where(lane < HEAD // 2, -1.0, 1.0)
    down = lax.broadcasted_iota(jnp.int32, (HEAD, HEAD), 0)
    across = lax.broadcasted_iota(jnp.int32, (HEAD, HEAD), 1)
    step = lax.broadcasted_iota(jnp.int32, (HEAD, 1), 0)
    reach = lax.broadcasted_iota(jnp.int32, (HEAD, BAND), 1)

    @pl.loop(0, ROWS // HEAD)
    def _(i):
        at = pl.multiple_of(i * HEAD, HEAD)
        here = b.segments[:, pl.ds(at, HEAD)].astype(jnp.float32)
        column = jnp.sum(jnp.where(down == across, here, 0.0), axis=1, keepdims=True)
        start = jnp.zeros_like(column)
        for v, count in enumerate(counts):
            start = start + jnp.where(column > v, count, 0.0)
        place_of = (step + at).astype(jnp.float32)
        angle = (place_of - start) * frequency
        b.cosine[pl.ds(at, HEAD), :] = jnp.cos(angle)
        b.sine[pl.ds(at, HEAD), :] = jnp.sin(angle) * sign
        key = (reach + ((i // 2) * QROWS + QROWS - BAND)).astype(jnp.float32)
        allowed = (key >= start) & (key <= place_of)
        b.bias[pl.ds(at, HEAD), :] = jnp.where(allowed, 0.0, MASKED)


def turned(b, raw, gain, at):
    scale = lax.rsqrt(jnp.mean(raw * raw, axis=-1, keepdims=True) + EPS)
    normed = raw * scale * gain
    turn = normed * b.cosine[at, :] + pltpu.roll(normed, HEAD // 2, 1) * b.sine[at, :]
    return turn.astype(jnp.bfloat16)


def chip_rows(k):
    s, _, _, _ = place()
    return pl.ds(pl.multiple_of((s // 2 + k) % SIDE * QROWS, QROWS), QROWS)


def project_keys(b, at):
    raw = jnp.dot(b.rows[at, :], b.wide.at[0].reshape(WIDTH, 2 * HEAD)[...], preferred_element_type=jnp.float32)
    b.keys[at, :] = turned(b, raw[:, :HEAD], b.k_gain[...], at)
    b.values[at, :] = raw[:, HEAD:].astype(jnp.bfloat16)


def keep_queries(b, raw, at):
    for h in range(raw.shape[1] // HEAD):
        b.queries[h, at, :] = turned(b, raw[:, h * HEAD : (h + 1) * HEAD], b.q_gain[...], at)


def project_queries(b, j, at):
    raw = jnp.dot(b.rows[at, :], b.wide.at[j].reshape(WIDTH, 2 * HEAD)[...], preferred_element_type=jnp.float32)
    keep_queries(b, raw, at)


FIRST_LINES, NEXT_LINES, LAST_LINES = (0,), (1, 3), (2,)


def lines_product(b, piece, at, steps):
    _, _, x, y = place()
    left_sides, right_sides = [], []
    for half, mine in ((0, y), (1, x)):
        for step in steps:
            line = half * SIDE + (mine + step) % SIDE
            left_sides.append(b.rows[at, pl.ds(pl.multiple_of(line * LINE, HEAD), LINE)])
            right_sides.append(piece[pl.ds(line * SIDE, SIDE)].reshape(LINE, piece.shape[-1]))
    return jnp.dot(
        jnp.concatenate(left_sides, axis=1), jnp.concatenate(right_sides, axis=0), preferred_element_type=jnp.float32
    )


def project_early(b, piece, partial):
    for i in range(ROWS // QROWS):
        at = pl.ds(i * QROWS, QROWS)
        partial[at, :] += lines_product(b, piece, at, NEXT_LINES)


def attend(b, heads, head, query):
    steps = ROWS // QROWS

    def reach_of(i):
        reach = min((i + 1) * QROWS, BAND)
        return reach, pl.ds((i + 1) * QROWS - reach, reach)

    def score(i):
        keys = b.keys[reach_of(i)[1], :]
        return lax.dot_general(query(i), keys, (((1,), (1,)), ((), ())), preferred_element_type=jnp.float32)

    def mix(i, scores):
        reach, keys = reach_of(i)
        bias = b.bias[pl.ds(i * QROWS, QROWS), BAND - reach :]
        weights = jnp.exp2(scores.reshape(heads, QROWS, reach) * SCALE + bias[None]).reshape(heads * QROWS, reach)
        total = jnp.sum(weights, axis=1, keepdims=True)
        mixed = jnp.dot(weights.astype(jnp.bfloat16), b.values[keys, :], preferred_element_type=jnp.float32)
        context = (mixed / total).astype(jnp.bfloat16).reshape(heads, QROWS // BLK, BLK, HEAD)
        for h in range(heads):
            b.context[h, pl.ds(i * (QROWS // BLK), QROWS // BLK)] = context[h]

    scores = score(0)
    for i in range(steps):
        later = score(i + 1) if i + 1 < steps else None
        mix(i, scores)
        scores = later

    per = BLOCKS // SEQ
    for h in range(heads):
        for t in range(SEQ):
            for r in range(per):
                b.send[head + h, t, pl.ds(r * BLK, BLK), :] = b.context[h, b.home[0, t * per + r]]
        send_context(b, head + h)


def attend_kept(b, head, slots):
    def query(i):
        at = pl.ds(i * QROWS, QROWS)
        parts = [b.queries[slot, at, :] for slot in slots]
        return parts[0] if len(parts) == 1 else jnp.concatenate(parts, axis=0)

    attend(b, len(slots), head, query)


def project_late(b, piece, partial):
    for i in range(ROWS // QROWS):
        at = pl.ds(i * QROWS, QROWS)
        keep_queries(b, partial[at, :] + lines_product(b, piece, at, LAST_LINES), at)


def barrier():
    s, d, _, _ = place()
    ready = pltpu.get_barrier_semaphore()
    for ring in range(2):
        for step in (1, -1):
            target, _ = along(ring, step)
            pl.semaphore_signal(ready, inc=1, device_id={"seq": s, "dp": target}, device_id_type=MESH)
    for step in range(1, SEQ):
        pl.semaphore_signal(ready, inc=1, device_id={"seq": (s + step) % SEQ, "dp": d}, device_id_type=MESH)
    pl.semaphore_wait(ready, 4 + SEQ - 1)


class Buffers:
    def __init__(self, names, refs):
        self.__dict__.update(zip(names, refs, strict=True))


SCRATCH = {
    "rows": pltpu.VMEM((ROWS, WIDTH), jnp.bfloat16),
    "wide": pltpu.VMEM((WIDE_CHUNKS + 1, PIECES, HALF, 2 * HEAD), jnp.bfloat16),
    "hidden_here": pltpu.VMEM((OWN, WIDTH), jnp.bfloat16),
    "segments": pltpu.VMEM((1, ROWS), jnp.int32),
    "home": pltpu.SMEM((1, BLOCKS), jnp.int32),
    "input_gain": pltpu.VMEM((1, WIDTH), jnp.float32),
    "q_gain": pltpu.VMEM((1, HEAD), jnp.float32),
    "k_gain": pltpu.VMEM((1, HEAD), jnp.float32),
    "cosine": pltpu.VMEM((ROWS, HEAD), jnp.float32),
    "sine": pltpu.VMEM((ROWS, HEAD), jnp.float32),
    "bias": pltpu.VMEM((ROWS, BAND), jnp.float32),
    "keys": pltpu.VMEM((ROWS, HEAD), jnp.bfloat16),
    "values": pltpu.VMEM((ROWS, HEAD), jnp.bfloat16),
    "queries": pltpu.VMEM((2, ROWS, HEAD), jnp.bfloat16),
    "partial": pltpu.VMEM((WIDE_CHUNKS - 1, ROWS, 2 * HEAD), jnp.float32),
    "context": pltpu.VMEM((2, BLOCKS, BLK, HEAD), jnp.bfloat16),
    "send": pltpu.VMEM((HEADS, SEQ, OWN, HEAD), jnp.bfloat16),
    "small": pltpu.SemaphoreType.DMA((6,)),
    "own": pltpu.SemaphoreType.DMA((CHUNKS,)),
    "weight_send": pltpu.SemaphoreType.DMA((CHUNKS,)),
    "weight_recv": pltpu.SemaphoreType.DMA((CHUNKS, 5)),
    "row_send": pltpu.SemaphoreType.DMA,
    "row_recv": pltpu.SemaphoreType.DMA((len(GROUPS),)),
    "twin_send": pltpu.SemaphoreType.DMA,
    "twin_recv": pltpu.SemaphoreType.DMA((len(GROUPS) + 1,)),
    "context_send": pltpu.SemaphoreType.DMA,
    "context_recv": pltpu.SemaphoreType.DMA,
    "context_own": pltpu.SemaphoreType.DMA,
}
OPERANDS = (
    "hidden",
    "segments_in",
    "home_in",
    "input_gain_in",
    "q_gain_in",
    "k_gain_in",
    "w_query",
    "key_weight",
    "value_weight",
    "out",
)


def kernel(*refs):
    b = Buffers(OPERANDS + tuple(SCRATCH), refs)
    small = [
        pltpu.make_async_copy(src, dst, b.small.at[i])
        for i, (src, dst) in enumerate(
            (
                (b.hidden.at[0], b.hidden_here),
                (b.input_gain_in, b.input_gain),
                (b.segments_in, b.segments),
                (b.home_in, b.home),
                (b.q_gain_in, b.q_gain),
                (b.k_gain_in, b.k_gain),
            )
        )
    ]
    for j in range(CHUNKS):
        begin_own(b, j)
        if j == 0:
            for copy in small:
                copy.start()
    barrier()

    for j in range(2):
        finish_own(b, j)
        begin_first(b, j)
    small[0].wait()
    small[1].wait()
    begin_rows(b)
    for j in range(2, CHUNKS):
        finish_own(b, j)
        begin_first(b, j)
    for copy in small[2:]:
        copy.wait()
    tables(b)
    for j in range(CHUNKS):
        pass_first(b, j)
    finish_first(b, 0)
    begin_second(b, 0, 0)
    begin_second(b, 0, 1)
    finish_first(b, 1)
    begin_second(b, 1, 0)
    for j in range(2, CHUNKS):
        finish_first(b, j)
    rows_arrived(b, 0)
    pass_second(b, 0)
    pass_second(b, 1)
    rows_arrived(b, 1)

    for part in range(2):
        finish_second(b, 0, part)
    for group in (len(GROUPS), 0, 1):
        twin_arrived(b, group)

    @pl.loop(0, SIDE - 1)
    def _(k):
        at = chip_rows((k + 3) % SIDE)
        project_keys(b, at)
        for j in (3, 4):
            b.partial[j - 2, at, :] = lines_product(b, b.wide.at[j], at, FIRST_LINES)

    pass_second(b, 2)
    for part in range(2):
        finish_second(b, 1, part)

    @pl.loop(0, SIDE - 1)
    def _(k):
        project_queries(b, 1, chip_rows((k + 3) % SIDE))

    finish_second(b, 2, 0)

    @pl.loop(0, SIDE - 1)
    def _(k):
        at = chip_rows((k + 3) % SIDE)
        b.partial[0, at, :] = lines_product(b, b.wide.at[2], at, FIRST_LINES + NEXT_LINES)

    for group in (2, 3):
        rows_arrived(b, group)
    for group in (2, 3):
        twin_arrived(b, group)
    project_keys(b, chip_rows(2))
    project_queries(b, 1, chip_rows(2))
    attend_kept(b, 0, (0,))
    attend_kept(b, 1, (1,))

    pass_second(b, 3)
    finish_second(b, 2, 1)
    for k in (3, 0, 1):
        at = chip_rows(k)
        keep_queries(b, b.partial[0, at, :] + lines_product(b, b.wide.at[2], at, LAST_LINES), at)
    project_queries(b, 2, chip_rows(2))
    attend_kept(b, 2, (0, 1))
    for j in (3, 4):
        at = chip_rows(2)
        b.partial[j - 2, at, :] = lines_product(b, b.wide.at[j], at, FIRST_LINES)

    finish_second(b, 3, 0)
    project_early(b, b.wide.at[3], b.partial.at[1])
    pass_second(b, 4)
    finish_second(b, 3, 1)
    project_late(b, b.wide.at[3], b.partial.at[1])
    attend_kept(b, 4, (0, 1))

    for j in range(WIDE_CHUNKS, CHUNKS):
        finish_second(b, j, 0)
        partial = b.partial.at[2, :, pl.ds((j - WIDE_CHUNKS) * HEAD, HEAD)]
        project_early(b, chunk(b, j), partial)
        if j + 1 < CHUNKS:
            pass_second(b, j + 1)
        finish_second(b, j, 1)
        project_late(b, chunk(b, j), partial)
        attend_kept(b, j + 2, (0,))

    for j in range(CHUNKS):
        left(b, chunk(b, j).at[pl.ds(0, PIECES - 2)], b.weight_send.at[j])
    left(b, b.rows.at[pl.ds(0, 6 * PIECE)], b.row_send)
    left(b, b.rows.at[pl.ds(0, OWN + 6 * PIECE)], b.twin_send)
    finish_context(b)


def hand_over(src, dst, sems):
    part = OWN // 4
    copies = [
        pltpu.make_async_copy(src.at[:, pl.ds(i * part, part)], dst.at[:, pl.ds(i * part, part)], sems.at[i])
        for i in range(4)
    ]
    for copy in copies:
        copy.start()
    for copy in copies:
        copy.wait()


def body(hidden_rows, segment_ids, block_home, input_gain, w_query, key_weight, value_weight, q_gain, k_gain):
    anywhere = pl.BlockSpec(memory_space=pl.ANY)
    vector = pl.BlockSpec(memory_space=pltpu.VMEM)
    shape = (1, OWN, SEQ * HEADS * HEAD)
    moved = pl.pallas_call(
        kernel,
        out_shape=pltpu.VMEM(shape, jnp.bfloat16),
        in_specs=[anywhere] * 9,
        out_specs=vector,
        scratch_shapes=list(SCRATCH.values()),
        compiler_params=pltpu.CompilerParams(
            collective_id=0, has_side_effects=True, vmem_limit_bytes=52 * 1024 * 1024
        ),
        name="packed_attention",
    )(
        hidden_rows,
        segment_ids,
        block_home,
        input_gain.reshape(1, WIDTH),
        q_gain.reshape(1, HEAD),
        k_gain.reshape(1, HEAD),
        w_query.reshape(2, HALF, HEADS * HEAD),
        key_weight.reshape(2, HALF, HEAD),
        value_weight.reshape(2, HALF, HEAD),
    )
    return pl.pallas_call(
        hand_over,
        out_shape=jax.ShapeDtypeStruct(shape, jnp.bfloat16),
        in_specs=[vector],
        out_specs=anywhere,
        scratch_shapes=[pltpu.SemaphoreType.DMA((4,))],
        compiler_params=pltpu.CompilerParams(vmem_limit_bytes=4 * 1024 * 1024),
        name="hand_over",
    )(moved)


def solution(mesh):
    return jax.shard_map(
        body,
        mesh=mesh,
        in_specs=(
            P("dp", "seq", None),
            P("dp", None),
            P("dp", None),
            P(),
            P("dp", "seq"),
            P("dp", "seq"),
            P("dp", "seq"),
            P(),
            P(),
        ),
        out_specs=P("dp", "seq", None),
        check_vma=False,
    )
```
